128 devices in a mesh: expert: 8 (over z, core), shard: 16 (over y, x).
Axes of the slice: x: 4, y: 4, z: 4, core: 2. Of those that a mesh axis runs over, the one named last changes fastest.
Arguments:
- tokens: bfloat16 [1024, 6144], P('expert'), may hold values from -6 to 6
- routes: int32 [1024, 2], P('expert'), may hold values from 0 to 7, all different within a row; in each aligned block of 128 rows (0 to 127, 128 to 255, ...) at most 64 rows name the same one
- route_weights: float32 [1024, 2], P('expert'), may hold values from 0.1 to 1
- out_grad: bfloat16 [1024, 6144], P('expert'), may hold values from -6 to 6
- w_gate: bfloat16 [8, 6144, 8192], P('expert', None, 'shard'), may hold values from -0.078125 to 0.078125
- w_up: bfloat16 [8, 6144, 8192], P('expert', None, 'shard'), may hold values from -0.078125 to 0.078125
- w_down: bfloat16 [8, 8192, 6144], P('expert', 'shard'), may hold values from -0.0625 to 0.0625
Outputs:
- moe_out: bfloat16 [1024, 6144], P('expert')
- input_grad: bfloat16 [1024, 6144], P('expert')
The draws below stay inside these ranges and needn't reach their ends.
Inputs may be any that keep to these rules, and one draw needn't show every extreme that they name: `routes`: the two experts of a token differ. In each aligned block of 128 rows (the tokens of one expert group) no expert is named by more than 64 rows, and in every draw some expert is named by exactly 64 rows of some block.
All inputs are finite; a program needn't handle non-finite values.
Results may differ from the reference program's by a relative error of at most 0.02.
Values may be sent and summed in bfloat16 or wider, within the bound.
No kernel may reach another device: no remote copies, remote signals or barrier semaphores. Data moves between devices by JAX's collectives and lax.ppermute only.
A program may use at most 128 MiB of HBM per device.

```python
import math
import jax
import jax.numpy as jnp
import numpy as np
from jax import lax

D = 6144
FF = 8192
TOK_DEV = 128
EXPERTS = 8
SHARDS = 16
TOKENS = 1024
MOST = 64
CAP = 512
FF_DEV = 512


def shard_levels(own_key, dims, shards, low, largest):
    level = 1.0
    for axis_at, parts in shards:
        heights = jax.random.uniform(jax.random.fold_in(jax.random.fold_in(own_key, 6), axis_at), (parts,), jnp.float32, low / len(shards), largest / len(shards))
        level = level * jnp.repeat(jnp.exp(heights), dims[axis_at] // parts).reshape((-1,) + (1,) * (len(dims) - 1 - axis_at))
    return level


def shared_out(key, own, number, rows, number_of, top, most, slope):
    sequence = jax.random.permutation(key, number_of)
    packed, usual = portions_of(number_of, rows * top, most, slope, True), portions_of(number_of, rows * top, most, slope, False)
    places = jnp.arange(number_of)

    def named(tallies, turn):
        used = int((tallies > 0).sum())
        fixed = max(1, used // 4)
        shifted = fixed + (places - fixed + turn * (used - fixed)) % max(1, number_of - fixed)
        return jnp.zeros((number_of,), jnp.int32).at[sequence[jnp.where(places < fixed, places, shifted)]].set(jnp.asarray(tallies, jnp.int32))

    tallies = jnp.where(number % 4 == 0, named(packed, number // 4), named(usual, number - number // 4 - 1))
    mixed = jax.random.permutation(jax.random.fold_in(own, 3), number_of)
    giver, taker = mixed[0:number_of // 2 * 2:2], mixed[1:number_of // 2 * 2:2]
    slack = jnp.minimum(tallies[giver] - 1, most - tallies[taker]) // 2
    slack = jnp.where((giver == sequence[0]) | (taker == sequence[0]) | (tallies[taker] == 0), 0, jnp.maximum(slack, 0))
    shifted = jax.random.randint(jax.random.fold_in(own, 4), (number_of // 2,), 0, 1 << 20) % (slack + 1)
    tallies = tallies.at[giver].add(-shifted).at[taker].add(shifted)
    items = jnp.searchsorted(jnp.cumsum(tallies), jnp.arange(rows * top), side="right").astype(jnp.int32)
    listing = items.reshape(top, rows).T
    listing = listing[jax.random.permutation(jax.random.fold_in(own, 1), rows)]
    turn = jax.random.randint(jax.random.fold_in(own, 2), (rows, 1), 0, top)
    return jnp.take_along_axis(listing, (jnp.arange(top)[None, :] + turn) % top, axis=1)


def portions_of(count, total, bound, slope, full):
    loads = [(1 << 20) // math.isqrt(standing ** slope) + 1 for standing in range(1, count + 1)]
    largest = bound if full else min(bound, max(-(-total // count), total * loads[0] // sum(loads)))
    least = 1 if total - largest >= count - 1 else 0
    given, rest = [largest] + [least] * (count - 1), total - largest - least * (count - 1)
    while rest > 0:
        candidates = [i for i in range(1, count) if given[i] < largest] or [i for i in range(1, count) if given[i] < bound]
        pool, left = sum([loads[i] for i in candidates]), rest
        for i in candidates:
            extra = min(bound - given[i], max(1, left * loads[i] // pool), rest)
            given[i] = given[i] + extra
            rest = rest - extra
    return np.array(given)


def bell_draw(own_key, dims, spread, most, shards=(), kind=jnp.bfloat16):
    gain = shard_levels(own_key, dims, shards, -0.22, 0.18) if shards else 1.0
    result = jax.random.normal(own_key, dims, jnp.float32) * spread * gain
    return jnp.minimum(jnp.maximum(result, -most), most).astype(kind)


def setup_inputs(seed: int = 0) -> dict:
    keys = jax.random.split(jax.random.key(seed), 8)
    tokens = bell_draw(keys[0], (TOKENS, D), 1.0, 6.0, ((0, 8),))
    routes_keys = jax.random.split(jax.random.fold_in(keys[1], 1), TOKENS // TOK_DEV)
    routes_turns = jax.random.permutation(jax.random.fold_in(keys[1], 3), TOKENS // TOK_DEV)
    routes = jax.vmap(lambda own, number: shared_out(jax.random.fold_in(keys[1], 2), own, number, TOK_DEV, EXPERTS, 2, MOST, 2))(routes_keys, routes_turns).reshape((TOKENS, 2))
    route_weights = jnp.clip(0.1 + 0.9 * jax.random.uniform(keys[2], (TOKENS, 2), jnp.float32) ** shard_levels(keys[2], (TOKENS, 2), ((0, 8),), -0.2, 0.2), 0.1, 1.0)
    out_grad = bell_draw(keys[3], (TOKENS, D), 1.0, 6.0, ((0, 8),))
    w_gate = bell_draw(keys[4], (EXPERTS, D, FF), D ** -0.5, 0.078125, ((0, 8), (2, 16)))
    w_up = bell_draw(keys[5], (EXPERTS, D, FF), D ** -0.5, 0.078125, ((0, 8), (2, 16)))
    w_down = bell_draw(keys[6], (EXPERTS, FF, D), FF ** -0.5, 0.0625, ((0, 8), (1, 16)))
    return {"tokens": tokens, "routes": routes, "route_weights": route_weights, "out_grad": out_grad, "w_gate": w_gate, "w_up": w_up, "w_down": w_down}


def reference(tokens, routes, route_weights, out_grad, w_gate, w_up, w_down):
    highest = lax.Precision.HIGHEST
    onehot = (routes[:, :, None] == jnp.arange(EXPERTS, dtype=jnp.int32)[None, None, :]).astype(jnp.int32)
    onehot = onehot.reshape(EXPERTS, 2 * TOK_DEV, EXPERTS)
    before = jnp.sum((jnp.cumsum(onehot, axis=1) - onehot) * onehot, axis=2).reshape(TOKENS, 2)
    block_id = (jnp.arange(TOKENS, dtype=jnp.int32) // TOK_DEV)[:, None]
    row_slot = (block_id * MOST + before).astype(jnp.int32)
    source = jnp.broadcast_to(jnp.arange(TOKENS, dtype=jnp.int32)[:, None], (TOKENS, 2)).reshape(-1)
    outputs = []
    gradients = []
    for expert in range(EXPERTS):
        target = jnp.where(routes == expert, row_slot, CAP).reshape(-1).astype(jnp.int32)
        rows_x = jnp.zeros((CAP, D), jnp.bfloat16).at[target].set(tokens[source], mode="drop")
        rows_g = jnp.zeros((CAP, D), jnp.bfloat16).at[target].set(out_grad[source], mode="drop")
        gate_w = w_gate[expert].astype(jnp.float32).reshape(D, SHARDS, FF_DEV)
        up_w = w_up[expert].astype(jnp.float32).reshape(D, SHARDS, FF_DEV)
        down_w = w_down[expert].astype(jnp.float32).reshape(SHARDS, FF_DEV, D)
        gate_act = jnp.einsum("rd,dsf->srf", rows_x.astype(jnp.float32), gate_w, precision=highest)
        up_act = jnp.einsum("rd,dsf->srf", rows_x.astype(jnp.float32), up_w, precision=highest)
        hidden = (jax.nn.silu(gate_act) * up_act).astype(jnp.bfloat16)
        pieces = jnp.einsum("srf,sfd->srd", hidden.astype(jnp.float32), down_w, precision=highest).astype(jnp.bfloat16)
        pieces = lax.optimization_barrier(pieces)
        outputs.append(jnp.sum(pieces.astype(jnp.float32), axis=0).astype(jnp.bfloat16))
        d_hidden = jnp.einsum("rd,sfd->srf", rows_g.astype(jnp.float32), down_w, precision=highest)
        sigmoid_g = jax.nn.sigmoid(gate_act)
        d_gate = (d_hidden * up_act * sigmoid_g * (1.0 + gate_act * (1.0 - sigmoid_g))).astype(jnp.bfloat16)
        d_up = (d_hidden * gate_act * sigmoid_g).astype(jnp.bfloat16)
        grad_pieces = jnp.einsum("srf,dsf->srd", d_gate.astype(jnp.float32), gate_w, precision=highest)
        grad_pieces = grad_pieces + jnp.einsum("srf,dsf->srd", d_up.astype(jnp.float32), up_w, precision=highest)
        grad_pieces = lax.optimization_barrier(grad_pieces.astype(jnp.bfloat16))
        gradients.append(jnp.sum(grad_pieces.astype(jnp.float32), axis=0).astype(jnp.bfloat16))
    stacked_out = jnp.stack(outputs)
    stacked_grad = jnp.stack(gradients)
    picked_out = stacked_out[routes, row_slot].astype(jnp.float32)
    picked_grad = stacked_grad[routes, row_slot].astype(jnp.float32)
    moe_out = jnp.sum(route_weights[:, :, None] * picked_out, axis=1).astype(jnp.bfloat16)
    input_grad = jnp.sum(route_weights[:, :, None] * picked_grad, axis=1).astype(jnp.bfloat16)
    return moe_out, input_grad
```

```python
import jax
import jax.numpy as jnp
from jax import lax
from jax.sharding import Mesh
from jax.sharding import PartitionSpec as P

CONTRACT_LAST = (((1,), (1,)), ((), ()))
F32 = jnp.float32
BF16 = jnp.bfloat16
EXPERT = ("z", "core")
RING = 4


def shift(rows, axis, step):
    return lax.ppermute(rows, axis, [(i, (i + step) % RING) for i in range(RING)])


def slots_of(routes, per_expert):
    flat = routes.reshape(-1)
    order = jnp.arange(flat.shape[0], dtype=jnp.int32)
    earlier = (flat[:, None] == flat[None, :]) & (order[:, None] > order[None, :])
    before = jnp.sum(earlier.astype(jnp.int32), axis=1)
    return (flat * per_expert + before).reshape(routes.shape)


def gathered(own, axis):
    half = own.shape[0] // 2
    before = shift(own, axis, 1)
    after = shift(own, axis, -1)
    top = shift(before[:half], axis, 1)
    bottom = shift(after[half:], axis, -1)
    return own, after, jnp.concatenate([top, bottom], axis=0), before


def summed(parts, axis):
    rows_at = parts[0].ndim - 2
    half = parts[0].shape[rows_at] // 2

    def pad(rows, front):
        widths = [(0, 0)] * rows.ndim
        widths[rows_at] = (half, 0) if front else (0, half)
        return jnp.pad(rows, widths).astype(F32)

    top = shift(lax.slice_in_dim(parts[2], 0, half, axis=rows_at).astype(BF16), axis, 1)
    bottom = shift(lax.slice_in_dim(parts[2], half, 2 * half, axis=rows_at).astype(BF16), axis, -1)
    plus = shift((parts[1].astype(F32) + pad(top, False)).astype(BF16), axis, 1)
    minus = shift((parts[3].astype(F32) + pad(bottom, True)).astype(BF16), axis, -1)
    return (parts[0].astype(F32) + plus.astype(F32) + minus.astype(F32)).astype(BF16)


def per_device(tokens, routes, route_weights, out_grad, w_gate, w_up, w_down):
    count_rows, width = tokens.shape
    groups = 8
    per_expert = 4 * count_rows // groups
    half = per_expert // 2
    chunk = width // RING
    part = chunk // RING
    w_gate, w_up, w_down = w_gate[0], w_up[0], w_down[0]
    axes = ("x", "y")
    place = [lax.axis_index(axis) for axis in axes]
    target = slots_of(routes, per_expert)
    slots = jnp.arange(groups * per_expert, dtype=jnp.int32).reshape(groups, 2, half)

    def send(rows):
        placed = []
        for h in range(2):
            own = slots[:, h].reshape(-1, 1)
            dispatch = ((own == target[None, :, 0]) | (own == target[None, :, 1])).astype(BF16)
            columns = lax.dynamic_slice_in_dim(rows, place[h] * chunk, chunk, axis=1)
            placed.append(jnp.dot(dispatch, columns, preferred_element_type=F32).astype(BF16))
        both = jnp.stack([p.reshape(groups, half, chunk) for p in placed], axis=1)
        got = lax.all_to_all(both, EXPERT, split_axis=0, concat_axis=0, tiled=True)
        return [gathered(got[:, h].reshape(groups * half, chunk), axes[h]) for h in range(2)]

    def row_chunk(weights, h, r):
        return lax.dynamic_slice_in_dim(weights, (place[h] + r) % RING * chunk, chunk, axis=0)

    def column_chunk(weights, h, r):
        return lax.dynamic_slice_in_dim(weights, (place[h] + r) % RING * chunk, chunk, axis=1)

    def piece_start(h, r, j):
        at = (place[h] + r) % RING
        return (at * RING + j if h == 0 else j * RING + at) * part

    def go_home(parts, h):
        total = summed(parts, axes[h])
        other = axes[1 - h]
        return lax.all_to_all(
            total.reshape(RING * groups, half, part), (other, *EXPERT), split_axis=0, concat_axis=0, tiled=True
        )

    def finish(home):
        total = 0.0
        chosen = 0.0
        for h in range(2):
            own = jnp.broadcast_to(slots[None, :, h], (RING, groups, half)).reshape(1, -1)
            choose = jnp.concatenate([target[:, k : k + 1] == own for k in range(2)], axis=0).astype(BF16)
            chosen += jnp.dot(choose, home[h].reshape(-1, part), preferred_element_type=F32)
        for k in range(2):
            total += route_weights[:, k : k + 1] * chosen[k * count_rows : (k + 1) * count_rows]
        mixed = total.astype(BF16)
        copies = jnp.broadcast_to(mixed[None], (RING * RING, count_rows, part))
        back = lax.all_to_all(copies, axes, split_axis=0, concat_axis=0, tiled=True)
        return back.transpose(1, 0, 2).reshape(count_rows, width)

    rows_x = send(tokens)
    rows_g = send(out_grad)
    out_home, grad_home = [], []
    for h in range(2):
        gate = sum(jnp.dot(rows_x[h][r], row_chunk(w_gate, h, r), preferred_element_type=F32) for r in (0, 1, 3, 2))
        up = sum(jnp.dot(rows_x[h][r], row_chunk(w_up, h, r), preferred_element_type=F32) for r in (0, 1, 3, 2))
        sigmoid = jax.nn.sigmoid(gate)
        hidden = (gate * sigmoid * up).astype(BF16)
        parts = []
        for r in range(RING):
            parts.append(jnp.stack([
                jnp.dot(hidden, lax.dynamic_slice_in_dim(w_down, piece_start(h, r, j), part, axis=1), preferred_element_type=F32).astype(BF16)
                for j in range(RING)]))
        out_home.append(go_home(parts, h))
        d_hidden = sum(
            lax.dot_general(rows_g[h][r], column_chunk(w_down, h, r), CONTRACT_LAST, preferred_element_type=F32)
            for r in (0, 1, 3, 2))
        d_gate = (d_hidden * up * sigmoid * (1.0 + gate * (1.0 - sigmoid))).astype(BF16)
        d_up = (d_hidden * gate * sigmoid).astype(BF16)
        parts = []
        for r in range(RING):
            pieces = []
            for j in range(RING):
                at = piece_start(h, r, j)
                piece = lax.dot_general(d_gate, lax.dynamic_slice_in_dim(w_gate, at, part, axis=0), CONTRACT_LAST, preferred_element_type=F32)
                piece += lax.dot_general(d_up, lax.dynamic_slice_in_dim(w_up, at, part, axis=0), CONTRACT_LAST, preferred_element_type=F32)
                pieces.append(piece.astype(BF16))
            parts.append(jnp.stack(pieces))
        grad_home.append(go_home(parts, h))
    return finish(out_home), finish(grad_home)


def solution(mesh):
    fine = Mesh(mesh.devices.reshape(4, 2, 4, 4), ("z", "core", "y", "x"))
    row = P(EXPERT, None)
    wide = P(EXPERT, None, ("y", "x"))
    tall = P(EXPERT, ("y", "x"), None)
    return jax.shard_map(
        per_device,
        mesh=fine,
        in_specs=(row, row, row, row, wide, wide, tall),
        out_specs=(row, row),
        check_vma=False,
    )
```

```python
import functools

import jax
import jax.numpy as jnp
from jax import lax
from jax.experimental import pallas as pl
from jax.experimental.pallas import tpu as pltpu
from jax.sharding import Mesh
from jax.sharding import PartitionSpec as P

F32 = jnp.float32
BF16 = jnp.bfloat16
EXPERT = ("z", "core")
AXES = ("x", "y")
RING = 4
GROUPS = 8
ROWS = 256
MIB = 1 << 20


def shift(rows, axis, step):
    return lax.ppermute(rows, axis, [(i, (i + step) % RING) for i in range(RING)])


def dot(a, b):
    return jnp.dot(a, b, preferred_element_type=F32)


def dot_t(a, b):
    return lax.dot_general(a, b, (((1,), (1,)), ((), ())), preferred_element_type=F32)


def slots_of(routes, per_expert):
    flat = routes.reshape(-1)
    order = jnp.arange(flat.shape[0], dtype=jnp.int32)
    earlier = (flat[:, None] == flat[None, :]) & (order[:, None] > order[None, :])
    before = jnp.sum(earlier.astype(jnp.int32), axis=1)
    return (flat * per_expert + before).reshape(routes.shape)


def whole(shape):
    return pl.BlockSpec(shape, lambda *_: (0,) * len(shape))


def halves_kernel(*refs):
    for source, to in zip(refs[:4], refs[4:]):
        to[...] = source[...]


def gathered(owns):
    rows, chunk = owns[0].shape
    half = rows // 2
    befores = [shift(own, axis, 1) for own, axis in zip(owns, AXES)]
    afters = [shift(own, axis, -1) for own, axis in zip(owns, AXES)]
    top = pl.BlockSpec((half, chunk), lambda i: (0, 0))
    bottom = pl.BlockSpec((half, chunk), lambda i: (1, 0))
    send = pl.pallas_call(
        halves_kernel,
        out_shape=[jax.ShapeDtypeStruct((half, chunk), BF16)] * 4,
        grid=(1,),
        in_specs=[top, top, bottom, bottom],
        out_specs=[whole((half, chunk))] * 4,
        compiler_params=params(12),
        cost_estimate=cost(0, 16 * half * chunk),
        name="halves",
    )(*befores, *afters)
    near = [[owns[h], afters[h], befores[h]] for h in range(2)]
    far = [[shift(send[h], AXES[h], 1), shift(send[2 + h], AXES[h], -1)] for h in range(2)]
    return near, far


def forward_near_kernel(place, *refs):
    rows, (wg, wu), (gate, up) = refs[:6], refs[6:8], refs[8:]
    for h in range(2):
        for i in range(3):

            @pl.when((pl.program_id(0) == h) & (pl.program_id(1) == i))
            def _(h=h, i=i):
                block = rows[3 * h + i][...]
                for acc, w in ((gate, wg), (up, wu)):
                    value = dot(block, w[...])
                    acc[...] = value if i == 0 else acc[...] + value


def forward_far_kernel(place, *refs):
    rows, (wg, wu, gate, up), (hidden, to_gate, to_up) = refs[:4], refs[4:8], refs[8:]
    for h in range(2):

        @pl.when(pl.program_id(0) == h)
        def _(h=h):
            block = jnp.concatenate([rows[2 * h][...], rows[2 * h + 1][...]], axis=0)
            g = gate[...] + dot(block, wg[...])
            u = up[...] + dot(block, wu[...])
            s = 1.0 / (1.0 + jnp.exp(-g))
            hidden[...] = (g * s * u).astype(BF16)
            to_gate[...] = u * s * (1.0 + g * (1.0 - s))
            to_up[...] = g * s


STEPS = 8


def hidden_grad_kernel(rows, wd, to_gate, to_up, after, d_gate, d_up, acc):
    step = pl.program_id(0)
    for h in range(2):
        at = slice(h * ROWS, (h + 1) * ROWS)
        value = dot_t(rows[:, h].reshape(ROWS, rows.shape[-1]), wd[...])

        @pl.when(step == 0)
        def _(at=at, value=value):
            acc[at] = value

        @pl.when(step > 0)
        def _(at=at, value=value):
            acc[at] += value

    @pl.when(step == STEPS - 1)
    def _():
        d_gate[...] = (acc[...] * to_gate[...]).astype(BF16)
        d_up[...] = (acc[...] * to_up[...]).astype(BF16)


def params(mib):
    return pltpu.CompilerParams(vmem_limit_bytes=mib * MIB)


def cost(flops, moved):
    return pl.CostEstimate(flops=int(flops), bytes_accessed=int(moved), transcendentals=0)


def forward(place, near, far, w_gate, w_up):
    width, hid = w_gate.shape
    chunk = width // RING

    def weights(distance):
        return pl.BlockSpec((chunk, hid), lambda *at: ((at[-1][at[0]] + distance(at)) % RING, 0))

    def by_half(*_):
        return pl.BlockSpec((ROWS, hid), lambda *at: (at[0], 0))

    near_w = weights(lambda at: jnp.where(at[1] == 2, 3, at[1]))
    rows = near[0] + near[1]
    gate, up = pl.pallas_call(
        forward_near_kernel,
        out_shape=[jax.ShapeDtypeStruct((2 * ROWS, hid), F32)] * 2,
        grid_spec=pltpu.PrefetchScalarGridSpec(
            num_scalar_prefetch=1,
            grid=(2, 3),
            in_specs=[whole(r.shape) for r in rows] + [near_w, near_w],
            out_specs=[by_half()] * 2,
        ),
        compiler_params=params(32),
        cost_estimate=cost(6 * ROWS * width * hid, 3 * width * ROWS + 6 * width * hid),
        name="forward_near",
    )(place, *rows, w_gate, w_up)
    far_w = weights(lambda at: 2)
    rows = far[0] + far[1]
    return pl.pallas_call(
        forward_far_kernel,
        out_shape=[jax.ShapeDtypeStruct((2 * ROWS, hid), t) for t in (BF16, F32, F32)],
        grid_spec=pltpu.PrefetchScalarGridSpec(
            num_scalar_prefetch=1,
            grid=(2,),
            in_specs=[whole(r.shape) for r in rows] + [far_w, far_w, by_half(), by_half()],
            out_specs=[by_half()] * 3,
        ),
        compiler_params=params(32),
        cost_estimate=cost(2 * ROWS * width * hid, width * ROWS + 2 * width * hid + 20 * ROWS * hid),
        name="forward_far",
    )(place, *rows, w_gate, w_up, gate, up)


def hidden_grad(rows, w_down, to_gate, to_up, after):
    hid, width = w_down.shape
    count = 2 * ROWS
    block = width // STEPS
    rows = rows.reshape(GROUPS, 2, ROWS // GROUPS, width)
    return pl.pallas_call(
        hidden_grad_kernel,
        out_shape=[jax.ShapeDtypeStruct((count, hid), BF16)] * 2,
        grid=(STEPS,),
        in_specs=[
            pl.BlockSpec((*rows.shape[:3], block), lambda i: (0, 0, 0, i)),
            pl.BlockSpec((hid, block), lambda i: (0, i)),
            whole((count, hid)),
            whole((count, hid)),
            pl.BlockSpec(memory_space=pl.ANY),
        ],
        out_specs=[whole((count, hid))] * 2,
        scratch_shapes=[pltpu.VMEM((count, hid), F32)],
        compiler_params=params(32),
        cost_estimate=cost(2 * count * width * hid, 2 * width * count + 2 * width * hid),
        name="hidden_grad",
    )(rows, w_down, to_gate, to_up, after)


def order(i):
    return jnp.where(i == 0, 2, jnp.where(i == 1, 1, jnp.where(i == 2, 3, 0)))


def parts_kernel(terms, transposed, place, after, *refs):
    part = refs[-1].shape[-1]
    acts = refs[:terms]
    weights = refs[terms : 6 * terms]
    outs = refs[6 * terms :]
    mult = dot_t if transposed else dot

    def product(h, j):
        total = 0.0
        for t in range(terms):
            mine = weights[5 * t : 5 * t + 5]
            act = acts[t][h * ROWS : (h + 1) * ROWS, :]
            if h == 1:
                block = mine[1 + j][...]
            elif transposed:
                block = mine[0][j * part : (j + 1) * part, :]
            else:
                block = mine[0][:, j * part : (j + 1) * part]
            total += mult(act, block)
        return total.astype(BF16)

    top, bottom = slice(0, ROWS // 2), slice(ROWS // 2, ROWS)
    for step in range(4):

        @pl.when(pl.program_id(0) == step)
        def _(step=step):
            for h in range(2):
                plus, minus, plus_later, minus_later, own = outs[5 * h : 5 * h + 5]
                for j in range(RING):
                    value = product(h, j)
                    if step == 0:
                        plus[0, j] = value[top]
                        minus[0, j] = value[bottom]
                    elif step == 1:
                        plus_later[j] = value[top]
                        plus[0, j] = value[bottom]
                    elif step == 2:
                        minus[0, j] = value[top]
                        minus_later[j] = value[bottom]
                    else:
                        own[j] = value


def ring_parts(place, after, acts, weights, transposed):
    hid = acts[0].shape[1]
    width = weights[0].shape[0] if transposed else weights[0].shape[1]
    chunk, part = width // RING, width // RING // RING

    def block(size, index):
        if transposed:
            return pl.BlockSpec((size, hid), lambda i, place: (index(i, place), 0))
        return pl.BlockSpec((hid, size), lambda i, place: (0, index(i, place)))

    specs, args = [], []
    for w in weights:
        specs.append(block(chunk, lambda i, place: (place[0] + order(i)) % RING))
        args.append(w)
        for j in range(RING):
            specs.append(block(part, lambda i, place, j=j: j * RING + (place[1] + order(i)) % RING))
            args.append(w)
    half = (RING, ROWS // 2, part)
    shapes = [(2, *half), (2, *half), half, half, (RING, ROWS, part)]
    out_specs = [
        pl.BlockSpec((1, *half), lambda i, place: (jnp.minimum(i, 1), 0, 0, 0)),
        pl.BlockSpec((1, *half), lambda i, place: (jnp.where(i >= 2, 1, 0), 0, 0, 0)),
        whole(half),
        whole(half),
        whole((RING, ROWS, part)),
    ]
    outs = pl.pallas_call(
        functools.partial(parts_kernel, len(acts), transposed),
        out_shape=[jax.ShapeDtypeStruct(s, BF16) for s in shapes] * 2,
        grid_spec=pltpu.PrefetchScalarGridSpec(
            num_scalar_prefetch=1,
            grid=(4,),
            in_specs=[pl.BlockSpec(memory_space=pl.ANY)] + [whole(a.shape) for a in acts] + specs,
            out_specs=out_specs * 2,
        ),
        compiler_params=params(44),
        cost_estimate=cost(len(acts) * 4 * ROWS * width * hid, len(acts) * 4 * width * hid + 4 * ROWS * width),
        name="grad_parts" if transposed else "out_parts",
    )(place, after, *acts, *args)
    return outs[:5], outs[5:]


def later_kernel(*refs):
    for own, got, total in zip(refs[:4], refs[4:8], refs[8:]):
        total[...] = (own[...].astype(F32) + got[0].astype(F32)).astype(BF16)


def total_kernel(*refs):
    half = ROWS // 2
    for h in range(2):
        own, first_plus, first_minus, later_plus, later_minus = refs[5 * h : 5 * h + 5]
        total = refs[10 + h]
        top = own[:, :half].astype(F32) + later_plus[...].astype(F32) + first_minus[0].astype(F32)
        bottom = own[:, half:].astype(F32) + first_plus[0].astype(F32) + later_minus[...].astype(F32)
        total[:, :half] = top.astype(BF16)
        total[:, half:] = bottom.astype(BF16)


def ring_sums(parts):
    half = parts[0][2].shape
    full = parts[0][4].shape
    plus = [shift(p[0], axis, 1) for p, axis in zip(parts, AXES)]
    minus = [shift(p[1], axis, -1) for p, axis in zip(parts, AXES)]
    first = pl.BlockSpec((1, *half), lambda i: (0, 0, 0, 0))
    second = pl.BlockSpec((1, *half), lambda i: (1, 0, 0, 0))
    send = pl.pallas_call(
        later_kernel,
        out_shape=[jax.ShapeDtypeStruct(half, BF16)] * 4,
        grid=(1,),
        in_specs=[whole(half)] * 4 + [first] * 4,
        out_specs=[whole(half)] * 4,
        compiler_params=params(16),
        cost_estimate=cost(0, 24 * ROWS // 2 * full[0] * full[2]),
        name="ring_later",
    )(*[p[2] for p in parts], *[p[3] for p in parts], *plus, *minus)
    operands, specs = [], []
    for h in range(2):
        operands += [parts[h][4], plus[h], minus[h], shift(send[h], AXES[h], 1), shift(send[2 + h], AXES[h], -1)]
        specs += [whole(full), second, second, whole(half), whole(half)]
    totals = pl.pallas_call(
        total_kernel,
        out_shape=[jax.ShapeDtypeStruct(full, BF16)] * 2,
        grid=(1,),
        in_specs=specs,
        out_specs=[whole(full)] * 2,
        compiler_params=params(24),
        cost_estimate=cost(0, 16 * ROWS * full[0] * full[2]),
        name="ring_total",
    )(*operands)
    return totals, send


def per_device(tokens, routes, route_weights, out_grad, w_gate, w_up, w_down):
    count_rows, width = tokens.shape
    per_expert = 4 * count_rows // GROUPS
    half = per_expert // 2
    chunk = width // RING
    part = chunk // RING
    w_gate, w_up, w_down = w_gate[0], w_up[0], w_down[0]
    place = [lax.axis_index(axis) for axis in AXES]
    places = jnp.stack(place).astype(jnp.int32)
    target = slots_of(routes, per_expert)
    slots = jnp.arange(GROUPS * per_expert, dtype=jnp.int32).reshape(GROUPS, 2, half)

    def placed(rows, h):
        mine = slots if h is None else slots[:, h]
        mine = mine.reshape(-1, 1)
        dispatch = ((mine == target[None, :, 0]) | (mine == target[None, :, 1])).astype(BF16)
        return dot(dispatch, rows).astype(BF16)

    def to_experts(rows):
        return lax.all_to_all(rows, EXPERT, split_axis=0, concat_axis=0, tiled=True)

    def quarter(h):
        return lax.dynamic_slice_in_dim(tokens, place[h] * chunk, chunk, axis=1)

    def go_home(totals):
        homes = []
        for h in range(2):
            total = totals[h].reshape(RING * GROUPS, half, part)
            axes = (AXES[1 - h], *EXPERT)
            homes.append(lax.all_to_all(total, axes, split_axis=0, concat_axis=0, tiled=True))
        return homes

    def finish(home):
        total = 0.0
        chosen = 0.0
        for h in range(2):
            own = jnp.broadcast_to(slots[None, :, h], (RING, GROUPS, half)).reshape(1, -1)
            choose = jnp.concatenate([target[:, k : k + 1] == own for k in range(2)], axis=0).astype(BF16)
            chosen += dot(choose, home[h].reshape(-1, part))
        for k in range(2):
            total += route_weights[:, k : k + 1] * chosen[k * count_rows : (k + 1) * count_rows]
        return total.astype(BF16)

    def ordered(slices):
        return slices.transpose(1, 0, 2).reshape(count_rows, width)

    quarters = jnp.stack([placed(quarter(h), h).reshape(GROUPS, half, chunk) for h in range(2)], axis=1)
    got = to_experts(quarters)
    rows_g = to_experts(placed(out_grad, None))
    near, far = gathered([got[:, h].reshape(ROWS, chunk) for h in range(2)])
    hidden, to_gate, to_up = forward(places, near, far, w_gate, w_up)
    out_parts = ring_parts(places, places, [hidden], [w_down], False)
    out_totals, sent = ring_sums(out_parts)
    d_gate, d_up = hidden_grad(rows_g, w_down, to_gate, to_up, out_parts[1][4])
    grad_parts = ring_parts(places, sent[0], [d_gate, d_up], [w_gate, w_up], True)
    grad_totals, _ = ring_sums(grad_parts)
    moe_out = ordered(lax.all_gather(finish(go_home(out_totals)), AXES, axis=0))
    copies = jnp.broadcast_to(finish(go_home(grad_totals))[None], (RING * RING, count_rows, part))
    input_grad = ordered(lax.all_to_all(copies, AXES, split_axis=0, concat_axis=0, tiled=True))
    return moe_out, input_grad


def solution(mesh):
    fine = Mesh(mesh.devices.reshape(4, 2, 4, 4), ("z", "core", "y", "x"))
    row = P(EXPERT, None)
    wide = P(EXPERT, None, ("y", "x"))
    tall = P(EXPERT, ("y", "x"), None)
    return jax.shard_map(
        per_device,
        mesh=fine,
        in_specs=(row, row, row, row, wide, wide, tall),
        out_specs=(row, row),
        check_vma=False,
    )
```

```python
import jax
import jax.numpy as jnp
from jax import lax
from jax.experimental import pallas as pl
from jax.experimental.pallas import tpu as pltpu
from jax.sharding import Mesh
from jax.sharding import PartitionSpec as P

F32 = jnp.float32
BF16 = jnp.bfloat16
EXPERT = ("z", "core")
AXES = ("x", "y")
RING = 4
GROUPS = 8
ROWS = 256
MIB = 1 << 20


def shift(rows, axis, step):
    return lax.ppermute(rows, axis, [(i, (i + step) % RING) for i in range(RING)])


def dot(a, b):
    return jnp.dot(a, b, preferred_element_type=F32)


def dot_t(a, b):
    return lax.dot_general(a, b, (((1,), (1,)), ((), ())), preferred_element_type=F32)


def slots_of(routes, per_expert):
    flat = routes.reshape(-1)
    order = jnp.arange(flat.shape[0], dtype=jnp.int32)
    earlier = (flat[:, None] == flat[None, :]) & (order[:, None] > order[None, :])
    before = jnp.sum(earlier.astype(jnp.int32), axis=1)
    return (flat * per_expert + before).reshape(routes.shape)


def whole(shape):
    return pl.BlockSpec(shape, lambda *_: (0,) * len(shape))


def halves_kernel(*refs):
    for source, to in zip(refs[:4], refs[4:]):
        to[...] = source[...]


def gathered(owns):
    rows, chunk = owns[0].shape
    half = rows // 2
    befores = [shift(own, axis, 1) for own, axis in zip(owns, AXES)]
    afters = [shift(own, axis, -1) for own, axis in zip(owns, AXES)]
    top = pl.BlockSpec((half, chunk), lambda i: (0, 0))
    bottom = pl.BlockSpec((half, chunk), lambda i: (1, 0))
    send = pl.pallas_call(
        halves_kernel,
        out_shape=[jax.ShapeDtypeStruct((half, chunk), BF16)] * 4,
        grid=(1,),
        in_specs=[top, top, bottom, bottom],
        out_specs=[whole((half, chunk))] * 4,
        compiler_params=params(),
        cost_estimate=cost(0, 16 * half * chunk),
        name="halves",
    )(*befores, *afters)
    near = [[owns[h], afters[h], befores[h]] for h in range(2)]
    far = [[shift(send[h], AXES[h], 1), shift(send[2 + h], AXES[h], -1)] for h in range(2)]
    return near, far


def forward_near_kernel(place, *refs):
    rows, (wg, wu), (gate, up) = refs[:6], refs[6:8], refs[8:]
    for h in range(2):
        for i in range(3):

            @pl.when((pl.program_id(0) == h) & (pl.program_id(1) == i))
            def _(h=h, i=i):
                block = rows[3 * h + i][...]
                for acc, w in ((gate, wg), (up, wu)):
                    value = dot(block, w[...])
                    acc[...] = value if i == 0 else acc[...] + value


def emit(at_step, distance, place, outs, product):
    part = outs[4].shape[-1]
    top, bottom = slice(0, ROWS // 2), slice(ROWS // 2, ROWS)
    for h in range(2):
        plus, minus, plus_later, minus_later, own = outs[5 * h : 5 * h + 5]
        chunk = (place[h] + distance) % RING
        columns = [
            pl.multiple_of((chunk * RING + j if h == 0 else j * RING + chunk) * part, part) for j in range(RING)
        ]
        values = product(h, columns).astype(BF16)
        for j in range(RING):
            value = values[:, j * part : (j + 1) * part]
            if at_step == 0:
                plus[0, j] = value[top]
                minus[0, j] = value[bottom]
            elif at_step == 1:
                plus_later[j] = value[top]
                plus[0, j] = value[bottom]
            elif at_step == 2:
                minus[0, j] = value[top]
                minus_later[j] = value[bottom]
            else:
                own[j] = value


def emitted(width, before, more):
    part = width // RING // RING
    half = (RING, ROWS // 2, part)
    shapes = [(2 + more, *half), (2 + more, *half), half, half, (RING, ROWS, part)]
    specs = [
        pl.BlockSpec((1, *half), lambda i, place: (jnp.clip(i - before, 0, 1 + more), 0, 0, 0)),
        pl.BlockSpec((1, *half), lambda i, place: (jnp.clip(i - before - 1, 0, 1 + more), 0, 0, 0)),
        whole(half),
        whole(half),
        whole((RING, ROWS, part)),
    ]
    return [jax.ShapeDtypeStruct(s, BF16) for s in shapes] * 2, specs * 2


DISTANCES = (2, 1, 3, 0)


def forward_far_kernel(place, *refs):
    rows, (wg, wu, gate, up, wd), (to_gate, to_up) = refs[:4], refs[4:9], refs[9:11]
    outs, (hidden, down, sem) = refs[11:21], refs[21:]
    step = pl.program_id(0)
    load = pltpu.make_async_copy(wd, down, sem)

    @pl.when(step == 0)
    def _():
        load.start()

    for h in range(2):

        @pl.when(step == h)
        def _(h=h):
            block = jnp.concatenate([rows[2 * h][...], rows[2 * h + 1][...]], axis=0)
            g = gate[...] + dot(block, wg[...])
            u = up[...] + dot(block, wu[...])
            s = 1.0 / (1.0 + jnp.exp(-g))
            hidden[h * ROWS : (h + 1) * ROWS] = (g * s * u).astype(BF16)
            to_gate[...] = u * s * (1.0 + g * (1.0 - s))
            to_up[...] = g * s

    @pl.when(step == 1)
    def _():
        load.wait()

    part = outs[4].shape[-1]

    def product(h, columns):
        weights = jnp.concatenate([down[:, pl.ds(at, part)] for at in columns], axis=1)
        return dot(hidden[h * ROWS : (h + 1) * ROWS], weights)

    for at_step, distance in enumerate(DISTANCES):

        @pl.when(step == 2 + at_step)
        def _(at_step=at_step, distance=distance):
            emit(at_step, distance, place, outs, product)


STEPS = 4


def backward_kernel(place, rows, wd, to_gate, to_up, wg, wu, *refs):
    waiting, outs, (acc, d_gate, d_up, gate, up, sems) = refs[:8], refs[8:18], refs[18:]
    step = pl.program_id(0)
    loads = [pltpu.make_async_copy(wg, gate, sems.at[0]), pltpu.make_async_copy(wu, up, sems.at[1])]

    @pl.when(step == 0)
    def _():
        for load in loads:
            load.start()

    @pl.when(step < STEPS)
    def _():
        value = dot_t(jnp.concatenate([rows[:, h].reshape(ROWS, rows.shape[-1]) for h in range(2)], axis=0), wd[...])

        @pl.when(step == 0)
        def _():
            acc[...] = value

        @pl.when(step > 0)
        def _():
            acc[...] += value

    @pl.when(step == STEPS - 1)
    def _():
        d_gate[...] = (acc[...] * to_gate[...]).astype(BF16)
        d_up[...] = (acc[...] * to_up[...]).astype(BF16)
        for load in loads:
            load.wait()

    part = outs[4].shape[-1]

    def product(h, columns):
        mine = slice(h * ROWS, (h + 1) * ROWS)
        gates, ups = (jnp.concatenate([w[pl.ds(at, part)] for at in columns], axis=0) for w in (gate, up))
        return dot_t(d_gate[mine], gates) + dot_t(d_up[mine], ups)

    for at_step, distance in enumerate(DISTANCES):

        @pl.when(step == STEPS + at_step)
        def _(at_step=at_step, distance=distance):
            emit(at_step, distance, place, outs, product)
            for h in range(2):
                if at_step >= 2:
                    own, got = waiting[2 * (at_step - 2) + h], waiting[4 + 2 * (at_step - 2) + h]
                    outs[5 * h + at_step - 2][0] = (own[...].astype(F32) + got[0].astype(F32)).astype(BF16)


def params(mib=58):
    return pltpu.CompilerParams(vmem_limit_bytes=mib * MIB)


def cost(flops, moved):
    return pl.CostEstimate(flops=int(flops), bytes_accessed=int(moved), transcendentals=0)


def forward(place, near, far, w_gate, w_up, w_down):
    width, hid = w_gate.shape
    chunk = width // RING

    def weights(distance):
        return pl.BlockSpec((chunk, hid), lambda *at: ((at[-1][at[0]] + distance(at)) % RING, 0))

    def by_half(*_):
        return pl.BlockSpec((ROWS, hid), lambda *at: (at[0], 0))

    near_w = weights(lambda at: jnp.where(at[1] == 2, 3, at[1]))
    rows = near[0] + near[1]
    gate, up = pl.pallas_call(
        forward_near_kernel,
        out_shape=[jax.ShapeDtypeStruct((2 * ROWS, hid), F32)] * 2,
        grid_spec=pltpu.PrefetchScalarGridSpec(
            num_scalar_prefetch=1,
            grid=(2, 3),
            in_specs=[whole(r.shape) for r in rows] + [near_w, near_w],
            out_specs=[by_half()] * 2,
        ),
        compiler_params=params(),
        cost_estimate=cost(6 * ROWS * width * hid, 3 * width * ROWS + 6 * width * hid),
        name="forward_near",
    )(place, *rows, w_gate, w_up)
    rows = far[0] + far[1]
    far_w = pl.BlockSpec((chunk, hid), lambda i, place: ((place[jnp.minimum(i, 1)] + 2) % RING, 0))
    half_rows = pl.BlockSpec((ROWS, hid), lambda i, place: (jnp.minimum(i, 1), 0))
    shapes, specs = emitted(width, 2, 0)
    outs = pl.pallas_call(
        forward_far_kernel,
        out_shape=[jax.ShapeDtypeStruct((2 * ROWS, hid), F32)] * 2 + shapes,
        grid_spec=pltpu.PrefetchScalarGridSpec(
            num_scalar_prefetch=1,
            grid=(6,),
            in_specs=[whole(r.shape) for r in rows]
            + [far_w, far_w, half_rows, half_rows, pl.BlockSpec(memory_space=pl.ANY)],
            out_specs=[half_rows] * 2 + specs,
            scratch_shapes=[
                pltpu.VMEM((2 * ROWS, hid), BF16),
                pltpu.VMEM((hid, width), BF16),
                pltpu.SemaphoreType.DMA,
            ],
        ),
        compiler_params=params(),
        cost_estimate=cost(6 * ROWS * width * hid, 2 * width * ROWS + 4 * width * hid + 16 * ROWS * hid),
        name="forward_far",
    )(place, *rows, w_gate, w_up, gate, up, w_down)
    return outs[0], outs[1], (outs[2:7], outs[7:])


def backward(place, rows, w_gate, w_up, w_down, to_gate, to_up, parts, first):
    hid, width = w_down.shape
    count = 2 * ROWS
    block = width // STEPS
    rows = rows.reshape(GROUPS, 2, ROWS // GROUPS, width)
    shapes, specs = emitted(width, STEPS, 1)
    anywhere = pl.BlockSpec(memory_space=pl.ANY)
    half = parts[0][2].shape
    waiting = [p[2] for p in parts] + [p[3] for p in parts]
    outs = pl.pallas_call(
        backward_kernel,
        out_shape=shapes,
        grid_spec=pltpu.PrefetchScalarGridSpec(
            num_scalar_prefetch=1,
            grid=(STEPS + 4,),
            in_specs=[
                pl.BlockSpec((*rows.shape[:3], block), lambda i, place: (0, 0, 0, jnp.minimum(i, STEPS - 1))),
                pl.BlockSpec((hid, block), lambda i, place: (0, jnp.minimum(i, STEPS - 1))),
                whole((count, hid)),
                whole((count, hid)),
                anywhere,
                anywhere,
            ]
            + [whole(half)] * 4
            + [pl.BlockSpec((1, *half), lambda i, place: (0, 0, 0, 0))] * 4,
            out_specs=specs,
            scratch_shapes=[
                pltpu.VMEM((count, hid), F32),
                pltpu.VMEM((count, hid), BF16),
                pltpu.VMEM((count, hid), BF16),
                pltpu.VMEM((width, hid), BF16),
                pltpu.VMEM((width, hid), BF16),
                pltpu.SemaphoreType.DMA((2,)),
            ],
        ),
        compiler_params=params(),
        cost_estimate=cost(6 * count * width * hid, 4 * width * count + 6 * width * hid),
        name="backward",
    )(place, rows, w_down, to_gate, to_up, w_gate, w_up, *waiting, *first)
    return outs[:5], outs[5:]


def combine_kernel(target, weights, *refs):
    homes, mixed = refs[:-1], refs[-1]
    tokens = target.shape[0]
    total = jnp.zeros((tokens, mixed.shape[-1]), F32)
    for h, home in enumerate(homes):
        at = lax.broadcasted_iota(jnp.int32, (tokens, home.shape[0]), 1)
        slot = ((at >> 5) & 7) * 64 + h * 32 + (at & 31)
        for k in range(2):
            choose = jnp.where(target[:, k : k + 1] == slot, 1.0, 0.0).astype(BF16)
            total += weights[:, k : k + 1] * dot(choose, home[...])
    for copy in range(mixed.shape[0]):
        mixed[copy] = total.astype(BF16)


def combine(homes, target, weights, copies):
    tokens = target.shape[0]
    part = homes[0].shape[-1]
    shape = (copies, tokens, part)
    return pl.pallas_call(
        combine_kernel,
        out_shape=jax.ShapeDtypeStruct(shape, BF16),
        grid=(1,),
        in_specs=[whole(target.shape), whole(weights.shape)] + [whole(h.shape) for h in homes],
        out_specs=whole(shape),
        compiler_params=params(),
        cost_estimate=cost(sum(4 * tokens * h.size for h in homes), 2 * (sum(h.size for h in homes) + copies * tokens * part)),
        name="combine",
    )(target, weights, *homes)


def add(*terms):
    return sum(t.astype(F32) for t in terms).astype(BF16)


def add_total(total, own, first_plus, first_minus, later_plus, later_minus):
    half = ROWS // 2
    total[:, :half] = add(own[:, :half], later_plus, first_minus)
    total[:, half:] = add(own[:, half:], first_plus, later_minus)


def middle_kernel(*refs):
    later, near, totals = refs[:8], refs[8:18], refs[22:]
    for own, got, send in zip(later[:4], later[4:], refs[18:22]):
        send[...] = add(own[...], got[0])
    for h in range(2):
        own, first_plus, first_minus, later_plus, later_minus = near[5 * h : 5 * h + 5]
        add_total(totals[h], own[...], first_plus[0], first_minus[0], later_plus[0], later_minus[0])


def total_kernel(after, *refs):
    for h in range(2):
        own, first_plus, first_minus, later_plus, later_minus = refs[5 * h : 5 * h + 5]
        add_total(refs[10 + h], own[...], first_plus[0], first_minus[0], later_plus[...], later_minus[...])


def both_ways(plus, minus):
    return [shift(p, axis, 1) for p, axis in zip(plus, AXES)] + [shift(m, axis, -1) for m, axis in zip(minus, AXES)]


def ring_middle(parts, got, out_parts, out_first):
    half, full = parts[0][2].shape, parts[0][4].shape
    blocks = [pl.BlockSpec((1, *half), lambda i, n=n: (n, 0, 0, 0)) for n in range(3)]
    operands = [p[2] for p in parts] + [p[3] for p in parts] + got
    specs = [whole(half)] * 4 + [blocks[0]] * 4
    for h in range(2):
        operands += [out_parts[h][4], out_first[h], out_first[2 + h], got[h], got[2 + h]]
        specs += [whole(full), blocks[1], blocks[1], blocks[2], blocks[2]]
    outs = pl.pallas_call(
        middle_kernel,
        out_shape=[jax.ShapeDtypeStruct(half, BF16)] * 4 + [jax.ShapeDtypeStruct(full, BF16)] * 2,
        grid=(1,),
        in_specs=specs,
        out_specs=[whole(half)] * 4 + [whole(full)] * 2,
        compiler_params=params(),
        cost_estimate=cost(0, 28 * ROWS * full[0] * full[2]),
        name="ring_middle",
    )(*operands)
    return outs[:4], outs[4:]


def ring_end(parts, first, later, after):
    half, full = parts[0][2].shape, parts[0][4].shape
    second = pl.BlockSpec((1, *half), lambda i: (1, 0, 0, 0))
    operands, specs = [after], [pl.BlockSpec(memory_space=pl.ANY)]
    for h in range(2):
        operands += [parts[h][4], first[h], first[2 + h], later[h], later[2 + h]]
        specs += [whole(full), second, second, whole(half), whole(half)]
    return pl.pallas_call(
        total_kernel,
        out_shape=[jax.ShapeDtypeStruct(full, BF16)] * 2,
        grid=(1,),
        in_specs=specs,
        out_specs=[whole(full)] * 2,
        compiler_params=params(),
        cost_estimate=cost(0, 16 * ROWS * full[0] * full[2]),
        name="ring_end",
    )(*operands)


def per_device(tokens, routes, route_weights, out_grad, w_gate, w_up, w_down):
    count_rows, width = tokens.shape
    per_expert = 4 * count_rows // GROUPS
    half = per_expert // 2
    chunk = width // RING
    part = chunk // RING
    w_gate, w_up, w_down = w_gate[0], w_up[0], w_down[0]
    place = [lax.axis_index(axis) for axis in AXES]
    places = jnp.stack(place).astype(jnp.int32)
    target = slots_of(routes, per_expert)
    slots = jnp.arange(GROUPS * per_expert, dtype=jnp.int32).reshape(GROUPS, 2, half)

    def placed(rows, h):
        mine = slots if h is None else slots[:, h]
        mine = mine.reshape(-1, 1)
        dispatch = ((mine == target[None, :, 0]) | (mine == target[None, :, 1])).astype(BF16)
        return dot(dispatch, rows).astype(BF16)

    def to_experts(rows):
        return lax.all_to_all(rows, EXPERT, split_axis=0, concat_axis=0, tiled=True)

    def quarter(h):
        return lax.dynamic_slice_in_dim(tokens, place[h] * chunk, chunk, axis=1)

    def go_home(totals):
        homes = []
        for h in range(2):
            total = totals[h].reshape(RING * GROUPS, half, part)
            axes = (AXES[1 - h], *EXPERT)
            homes.append(lax.all_to_all(total, axes, split_axis=0, concat_axis=0, tiled=True))
        return homes

    def ordered(slices):
        return slices.transpose(1, 0, 2).reshape(count_rows, width)

    quarters = jnp.stack([placed(quarter(h), h).reshape(GROUPS, half, chunk) for h in range(2)], axis=1)
    got = to_experts(quarters)
    rows_g = to_experts(placed(out_grad, None))
    near, far = gathered([got[:, h].reshape(ROWS, chunk) for h in range(2)])
    to_gate, to_up, out_parts = forward(places, near, far, w_gate, w_up, w_down)
    out_first = both_ways([p[0] for p in out_parts], [p[1] for p in out_parts])
    grad_parts = backward(places, rows_g, w_gate, w_up, w_down, to_gate, to_up, out_parts, out_first)
    got = both_ways([p[0] for p in grad_parts], [p[1] for p in grad_parts])
    send, out_totals = ring_middle(grad_parts, got, out_parts, out_first)
    grad_later = both_ways(send[:2], send[2:])
    mixed = combine([h.reshape(-1, part) for h in go_home(out_totals)], target, route_weights, 1)[0]
    moe_out = ordered(lax.all_gather(mixed, AXES, axis=0))
    grad_home = go_home(ring_end(grad_parts, got, grad_later, mixed))
    copies = combine([h.reshape(-1, part) for h in grad_home], target, route_weights, RING * RING)
    input_grad = ordered(lax.all_to_all(copies, AXES, split_axis=0, concat_axis=0, tiled=True))
    return moe_out, input_grad


def solution(mesh):
    fine = Mesh(mesh.devices.reshape(4, 2, 4, 4), ("z", "core", "y", "x"))
    row = P(EXPERT, None)
    wide = P(EXPERT, None, ("y", "x"))
    tall = P(EXPERT, ("y", "x"), None)
    return jax.shard_map(
        per_device,
        mesh=fine,
        in_specs=(row, row, row, row, wide, wide, tall),
        out_specs=(row, row),
        check_vma=False,
    )
```

```python
import jax
import jax.numpy as jnp
from jax import lax
from jax.experimental import pallas as pl
from jax.experimental.pallas import tpu as pltpu
from jax.sharding import Mesh
from jax.sharding import PartitionSpec as P

F32 = jnp.float32
BF16 = jnp.bfloat16
EXPERT = ("z", "core")
AXES = ("x", "y")
RING = 4
GROUPS = 8
ROWS = 256
MIB = 1 << 20


def shift(rows, axis, step):
    return lax.ppermute(rows, axis, [(i, (i + step) % RING) for i in range(RING)])


def dot(a, b):
    return jnp.dot(a, b, preferred_element_type=F32)


def dot_t(a, b):
    return lax.dot_general(a, b, (((1,), (1,)), ((), ())), preferred_element_type=F32)


def slots_of(routes, per_expert):
    flat = routes.reshape(-1)
    order = jnp.arange(flat.shape[0], dtype=jnp.int32)
    earlier = (flat[:, None] == flat[None, :]) & (order[:, None] > order[None, :])
    before = jnp.sum(earlier.astype(jnp.int32), axis=1)
    return (flat * per_expert + before).reshape(routes.shape)


def whole(shape):
    return pl.BlockSpec(shape, lambda *_: (0,) * len(shape))


def halves_kernel(*refs):
    for source, to in zip(refs[:4], refs[4:]):
        to[...] = source[...]


def gathered(owns):
    rows, chunk = owns[0].shape
    half = rows // 2
    befores = [shift(own, axis, 1) for own, axis in zip(owns, AXES)]
    afters = [shift(own, axis, -1) for own, axis in zip(owns, AXES)]
    top = pl.BlockSpec((half, chunk), lambda i: (0, 0))
    bottom = pl.BlockSpec((half, chunk), lambda i: (1, 0))
    send = pl.pallas_call(
        halves_kernel,
        out_shape=[jax.ShapeDtypeStruct((half, chunk), BF16)] * 4,
        grid=(1,),
        in_specs=[top, top, bottom, bottom],
        out_specs=[whole((half, chunk))] * 4,
        compiler_params=params(),
        cost_estimate=cost(0, 16 * half * chunk),
        name="halves",
    )(*befores, *afters)
    near = [[owns[h], afters[h], befores[h]] for h in range(2)]
    far = [[shift(send[h], AXES[h], 1), shift(send[2 + h], AXES[h], -1)] for h in range(2)]
    return near, far


def forward_near_kernel(place, *refs):
    rows, (wg, wu), (gate, up) = refs[:6], refs[6:8], refs[8:]
    for h in range(2):
        for i in range(3):

            @pl.when((pl.program_id(0) == h) & (pl.program_id(1) == i))
            def _(h=h, i=i):
                block = rows[3 * h + i][...]
                for acc, w in ((gate, wg), (up, wu)):
                    value = dot(block, w[...])
                    acc[...] = value if i == 0 else acc[...] + value


def emit(at_step, distance, place, outs, product):
    part = outs[4].shape[-1]
    top, bottom = slice(0, ROWS // 2), slice(ROWS // 2, ROWS)
    for h in range(2):
        plus, minus, plus_later, minus_later, own = outs[5 * h : 5 * h + 5]
        chunk = (place[h] + distance) % RING
        columns = [
            pl.multiple_of((chunk * RING + j if h == 0 else j * RING + chunk) * part, part) for j in range(RING)
        ]
        values = product(h, columns).astype(BF16)
        for j in range(RING):
            value = values[:, j * part : (j + 1) * part]
            if at_step == 0:
                plus[0, j] = value[top]
                minus[0, j] = value[bottom]
            elif at_step == 1:
                plus_later[j] = value[top]
                plus[0, j] = value[bottom]
            elif at_step == 2:
                minus[0, j] = value[top]
                minus_later[j] = value[bottom]
            else:
                own[j] = value


def emitted(width, before, more):
    part = width // RING // RING
    half = (RING, ROWS // 2, part)
    shapes = [(2 + more, *half), (2 + more, *half), half, half, (RING, ROWS, part)]
    specs = [
        pl.BlockSpec((1, *half), lambda i, place: (jnp.clip(i - before, 0, 1), 0, 0, 0)),
        pl.BlockSpec((1, *half), lambda i, place: (jnp.clip(i - before - 1, 0, 1), 0, 0, 0)),
        whole(half),
        whole(half),
        whole((RING, ROWS, part)),
    ]
    return [jax.ShapeDtypeStruct(s, BF16) for s in shapes] * 2, specs * 2


DISTANCES = (2, 1, 3, 0)


def forward_far_kernel(place, *refs):
    rows, (wg, wu, gate, up, wd), (to_gate, to_up) = refs[:4], refs[4:9], refs[9:11]
    outs, (hidden, down, sem) = refs[11:21], refs[21:]
    step = pl.program_id(0)
    load = pltpu.make_async_copy(wd, down, sem)

    @pl.when(step == 0)
    def _():
        load.start()

    for h in range(2):

        @pl.when(step == h)
        def _(h=h):
            block = jnp.concatenate([rows[2 * h][...], rows[2 * h + 1][...]], axis=0)
            g = gate[...] + dot(block, wg[...])
            u = up[...] + dot(block, wu[...])
            s = 1.0 / (1.0 + jnp.exp(-g))
            hidden[h * ROWS : (h + 1) * ROWS] = (g * s * u).astype(BF16)
            to_gate[...] = u * s * (1.0 + g * (1.0 - s))
            to_up[...] = g * s

    @pl.when(step == 1)
    def _():
        load.wait()

    part = outs[4].shape[-1]

    def product(h, columns):
        weights = jnp.concatenate([down[:, pl.ds(at, part)] for at in columns], axis=1)
        return dot(hidden[h * ROWS : (h + 1) * ROWS], weights)

    for at_step, distance in enumerate(DISTANCES):

        @pl.when(step == 2 + at_step)
        def _(at_step=at_step, distance=distance):
            emit(at_step, distance, place, outs, product)


STEPS = 4


def backward_kernel(place, rows, wd, to_gate, to_up, wg, wu, *refs):
    outs, (acc, d_gate, d_up, gate, up, sems) = refs[:10], refs[10:]
    step = pl.program_id(0)
    loads = [pltpu.make_async_copy(wg, gate, sems.at[0]), pltpu.make_async_copy(wu, up, sems.at[1])]

    @pl.when(step == 0)
    def _():
        for load in loads:
            load.start()

    @pl.when(step < STEPS)
    def _():
        value = dot_t(jnp.concatenate([rows[:, h].reshape(ROWS, rows.shape[-1]) for h in range(2)], axis=0), wd[...])

        @pl.when(step == 0)
        def _():
            acc[...] = value

        @pl.when(step > 0)
        def _():
            acc[...] += value

    @pl.when(step == STEPS - 1)
    def _():
        d_gate[...] = (acc[...] * to_gate[...]).astype(BF16)
        d_up[...] = (acc[...] * to_up[...]).astype(BF16)
        for load in loads:
            load.wait()

    part = outs[4].shape[-1]

    def product(h, columns):
        mine = slice(h * ROWS, (h + 1) * ROWS)
        gates, ups = (jnp.concatenate([w[pl.ds(at, part)] for at in columns], axis=0) for w in (gate, up))
        return dot_t(d_gate[mine], gates) + dot_t(d_up[mine], ups)

    for at_step, distance in enumerate(DISTANCES):

        @pl.when(step == STEPS + at_step)
        def _(at_step=at_step, distance=distance):
            emit(at_step, distance, place, outs, product)


def params(mib=58):
    return pltpu.CompilerParams(vmem_limit_bytes=mib * MIB)


def cost(flops, moved):
    return pl.CostEstimate(flops=int(flops), bytes_accessed=int(moved), transcendentals=0)


def forward(place, near, far, w_gate, w_up, w_down):
    width, hid = w_gate.shape
    chunk = width // RING

    def weights(distance):
        return pl.BlockSpec((chunk, hid), lambda *at: ((at[-1][at[0]] + distance(at)) % RING, 0))

    def by_half(*_):
        return pl.BlockSpec((ROWS, hid), lambda *at: (at[0], 0))

    near_w = weights(lambda at: jnp.where(at[1] == 2, 3, at[1]))
    rows = near[0] + near[1]
    gate, up = pl.pallas_call(
        forward_near_kernel,
        out_shape=[jax.ShapeDtypeStruct((2 * ROWS, hid), F32)] * 2,
        grid_spec=pltpu.PrefetchScalarGridSpec(
            num_scalar_prefetch=1,
            grid=(2, 3),
            in_specs=[whole(r.shape) for r in rows] + [near_w, near_w],
            out_specs=[by_half()] * 2,
        ),
        compiler_params=params(),
        cost_estimate=cost(6 * ROWS * width * hid, 3 * width * ROWS + 6 * width * hid),
        name="forward_near",
    )(place, *rows, w_gate, w_up)
    rows = far[0] + far[1]
    far_w = pl.BlockSpec((chunk, hid), lambda i, place: ((place[jnp.minimum(i, 1)] + 2) % RING, 0))
    half_rows = pl.BlockSpec((ROWS, hid), lambda i, place: (jnp.minimum(i, 1), 0))
    shapes, specs = emitted(width, 2, 0)
    outs = pl.pallas_call(
        forward_far_kernel,
        out_shape=[jax.ShapeDtypeStruct((2 * ROWS, hid), F32)] * 2 + shapes,
        grid_spec=pltpu.PrefetchScalarGridSpec(
            num_scalar_prefetch=1,
            grid=(6,),
            in_specs=[whole(r.shape) for r in rows]
            + [far_w, far_w, half_rows, half_rows, pl.BlockSpec(memory_space=pl.ANY)],
            out_specs=[half_rows] * 2 + specs,
            scratch_shapes=[
                pltpu.VMEM((2 * ROWS, hid), BF16),
                pltpu.VMEM((hid, width), BF16),
                pltpu.SemaphoreType.DMA,
            ],
        ),
        compiler_params=params(),
        cost_estimate=cost(6 * ROWS * width * hid, 2 * width * ROWS + 4 * width * hid + 16 * ROWS * hid),
        name="forward_far",
    )(place, *rows, w_gate, w_up, gate, up, w_down)
    return outs[0], outs[1], (outs[2:7], outs[7:])


def backward(place, rows, w_gate, w_up, w_down, to_gate, to_up):
    hid, width = w_down.shape
    count = 2 * ROWS
    block = width // STEPS
    rows = rows.reshape(GROUPS, 2, ROWS // GROUPS, width)
    shapes, specs = emitted(width, STEPS, 1)
    anywhere = pl.BlockSpec(memory_space=pl.ANY)
    outs = pl.pallas_call(
        backward_kernel,
        out_shape=shapes,
        grid_spec=pltpu.PrefetchScalarGridSpec(
            num_scalar_prefetch=1,
            grid=(STEPS + 4,),
            in_specs=[
                pl.BlockSpec((*rows.shape[:3], block), lambda i, place: (0, 0, 0, jnp.minimum(i, STEPS - 1))),
                pl.BlockSpec((hid, block), lambda i, place: (0, jnp.minimum(i, STEPS - 1))),
                whole((count, hid)),
                whole((count, hid)),
                anywhere,
                anywhere,
            ],
            out_specs=specs,
            scratch_shapes=[
                pltpu.VMEM((count, hid), F32),
                pltpu.VMEM((count, hid), BF16),
                pltpu.VMEM((count, hid), BF16),
                pltpu.VMEM((width, hid), BF16),
                pltpu.VMEM((width, hid), BF16),
                pltpu.SemaphoreType.DMA((2,)),
            ],
        ),
        compiler_params=params(),
        cost_estimate=cost(6 * count * width * hid, 4 * width * count + 6 * width * hid),
        name="backward",
    )(place, rows, w_down, to_gate, to_up, w_gate, w_up)
    return outs[:5], outs[5:]


def combine_kernel(target, weights, *refs):
    homes, mixed = refs[:-1], refs[-1]
    tokens, part = mixed.shape[2:]
    totals = [jnp.zeros((tokens, part), F32) for _ in range(2)]
    for h, home in enumerate(homes):
        rows = [home[:, n].reshape(-1, part) for n in range(2)]
        at = lax.broadcasted_iota(jnp.int32, (tokens, rows[0].shape[0]), 1)
        slot = ((at >> 5) & 7) * 64 + h * 32 + (at & 31)
        for k in range(2):
            choose = jnp.where(target[:, k : k + 1] == slot, 1.0, 0.0).astype(BF16)
            for n in range(2):
                totals[n] += weights[:, k : k + 1] * dot(choose, rows[n])
    for n in range(2):
        for copy in range(mixed.shape[0]):
            mixed[copy, n] = totals[n].astype(BF16)


def combine(homes, target, weights, copies):
    tokens = target.shape[0]
    shape = (copies, 2, tokens, homes[0].shape[-1])
    return pl.pallas_call(
        combine_kernel,
        out_shape=jax.ShapeDtypeStruct(shape, BF16),
        grid=(1,),
        in_specs=[whole(target.shape), whole(weights.shape)] + [whole(h.shape) for h in homes],
        out_specs=whole(shape),
        compiler_params=params(),
        cost_estimate=cost(8 * tokens * homes[0].size, 4 * homes[0].size + 4 * copies * tokens * shape[-1]),
        name="combine",
    )(target, weights, *homes)


def add(*terms):
    return sum(t.astype(F32) for t in terms).astype(BF16)


def later_kernel(*refs):
    for own, got, send in zip(refs[:4], refs[4:8], refs[-4:]):
        send[...] = add(own[...], got[0]).reshape(send.shape)


def total_kernel(*refs):
    half = ROWS // 2
    for n in range(2):
        for h in range(2):
            own, first_plus, first_minus, later_plus, later_minus = (r[...] for r in refs[10 * n + 5 * h : 10 * n + 5 * h + 5])
            own = own[0]
            first_plus, first_minus, later_plus, later_minus = (
                r.reshape(half, r.shape[-1]) for r in (first_plus, first_minus, later_plus, later_minus)
            )
            top = add(own[:half], later_plus, first_minus)
            bottom = add(own[half:], first_plus, later_minus)
            total = refs[20 + h]
            shape = (GROUPS // 2, *total.shape[3:])
            total[0, : GROUPS // 2, n] = top.reshape(shape)
            total[0, GROUPS // 2 :, n] = bottom.reshape(shape)


def both_ways(plus, minus):
    return [shift(p, axis, 1) for p, axis in zip(plus, AXES)] + [shift(m, axis, -1) for m, axis in zip(minus, AXES)]


def ring_join(parts, first, plus, minus):
    half = parts[0][2].shape
    block = pl.BlockSpec((1, *half), lambda i: (0, 0, 0, 0))
    third = pl.BlockSpec((1, *half), lambda i: (2, 0, 0, 0))
    buffers = [*plus, *minus]
    outs = pl.pallas_call(
        later_kernel,
        out_shape=[jax.ShapeDtypeStruct(b.shape, BF16) for b in buffers],
        grid=(1,),
        in_specs=[whole(half)] * 4 + [block] * 4 + [pl.BlockSpec(memory_space=pl.ANY)] * 4,
        out_specs=[third] * 4,
        input_output_aliases={8 + n: n for n in range(4)},
        compiler_params=params(),
        cost_estimate=cost(0, 24 * half[0] * half[1] * half[2]),
        name="ring_join",
    )(*[p[2] for p in parts], *[p[3] for p in parts], *first, *buffers)
    return outs[:2], outs[2:]


def ring_later(parts, first):
    half = parts[0][2].shape
    block = pl.BlockSpec((1, *half), lambda i: (0, 0, 0, 0))
    outs = pl.pallas_call(
        later_kernel,
        out_shape=[jax.ShapeDtypeStruct(half, BF16)] * 4,
        grid=(1,),
        in_specs=[whole(half)] * 4 + [block] * 4,
        out_specs=[whole(half)] * 4,
        compiler_params=params(),
        cost_estimate=cost(0, 24 * half[0] * half[1] * half[2]),
        name="ring_later",
    )(*[p[2] for p in parts], *[p[3] for p in parts], *first)
    return outs[:2], outs[2:]


def ring_end(out_parts, out_first, got, grad_parts, grad_later):
    _, rows, part = out_parts[0][4].shape
    own = pl.BlockSpec((1, rows, part), lambda j: (j, 0, 0))
    blocks = [pl.BlockSpec((1, 1, rows // 2, part), lambda j, n=n: (n, j, 0, 0)) for n in range(3)]
    later = pl.BlockSpec((1, rows // 2, part), lambda j: (j, 0, 0))
    operands, specs = [], []
    for h in range(2):
        operands += [out_parts[h][4], out_first[h], out_first[2 + h], got[h], got[2 + h]]
        specs += [own, blocks[1], blocks[1], blocks[2], blocks[2]]
    for h in range(2):
        operands += [grad_parts[h][4], got[h], got[2 + h], grad_later[h], grad_later[2 + h]]
        specs += [own, blocks[1], blocks[1], later, later]
    shape = (RING, GROUPS, 2, rows // GROUPS, part)
    return pl.pallas_call(
        total_kernel,
        out_shape=[jax.ShapeDtypeStruct(shape, BF16)] * 2,
        grid=(RING,),
        in_specs=specs,
        out_specs=[pl.BlockSpec((1, *shape[1:]), lambda j: (j, 0, 0, 0, 0))] * 2,
        compiler_params=params(),
        cost_estimate=cost(0, 32 * RING * rows * part),
        name="ring_end",
    )(*operands)


def assemble_kernel(slices, *results):
    count, _, _, part = slices.shape
    for n, result in enumerate(results):
        for c in range(count):
            result[:, c * part : (c + 1) * part] = slices[c, n]


def assemble(slices):
    count, _, tokens, part = slices.shape
    return pl.pallas_call(
        assemble_kernel,
        out_shape=[jax.ShapeDtypeStruct((tokens, count * part), BF16)] * 2,
        grid=(RING,),
        in_specs=[pl.BlockSpec((count // RING, 2, tokens, part), lambda i: (i, 0, 0, 0))],
        out_specs=[pl.BlockSpec((tokens, count // RING * part), lambda i: (0, i))] * 2,
        compiler_params=params(),
        cost_estimate=cost(0, 4 * slices.size),
        name="assemble",
    )(slices)


def per_device(tokens, routes, route_weights, out_grad, w_gate, w_up, w_down):
    count_rows, width = tokens.shape
    per_expert = 4 * count_rows // GROUPS
    half = per_expert // 2
    chunk = width // RING
    part = chunk // RING
    w_gate, w_up, w_down = w_gate[0], w_up[0], w_down[0]
    place = [lax.axis_index(axis) for axis in AXES]
    places = jnp.stack(place).astype(jnp.int32)
    target = slots_of(routes, per_expert)
    slots = jnp.arange(GROUPS * per_expert, dtype=jnp.int32).reshape(GROUPS, 2, half)

    def placed(rows, h):
        mine = slots if h is None else slots[:, h]
        mine = mine.reshape(-1, 1)
        dispatch = ((mine == target[None, :, 0]) | (mine == target[None, :, 1])).astype(BF16)
        return dot(dispatch, rows).astype(BF16)

    def to_experts(rows):
        return lax.all_to_all(rows, EXPERT, split_axis=0, concat_axis=0, tiled=True)

    def quarter(h):
        return lax.dynamic_slice_in_dim(tokens, place[h] * chunk, chunk, axis=1)

    quarters = jnp.stack([placed(quarter(h), h).reshape(GROUPS, half, chunk) for h in range(2)], axis=1)
    got = to_experts(quarters)
    rows_g = to_experts(placed(out_grad, None))
    near, far = gathered([got[:, h].reshape(ROWS, chunk) for h in range(2)])
    to_gate, to_up, out_parts = forward(places, near, far, w_gate, w_up, w_down)
    out_first = both_ways([p[0] for p in out_parts], [p[1] for p in out_parts])
    grad_parts = backward(places, rows_g, w_gate, w_up, w_down, to_gate, to_up)
    plus, minus = ring_join(out_parts, out_first, [p[0] for p in grad_parts], [p[1] for p in grad_parts])
    got = both_ways(plus, minus)
    grad_later = both_ways(*ring_later(grad_parts, got))
    totals = ring_end(out_parts, out_first, got, grad_parts, grad_later)
    homes = []
    for h in range(2):
        pieces = totals[h].reshape(RING * GROUPS, 2, half, part)
        axes = (AXES[1 - h], *EXPERT)
        homes.append(lax.all_to_all(pieces, axes, split_axis=0, concat_axis=0, tiled=True))
    copies = combine(homes, target, route_weights, RING * RING)
    moe_out, input_grad = assemble(lax.all_to_all(copies, AXES, split_axis=0, concat_axis=0, tiled=True))
    return moe_out, input_grad


def solution(mesh):
    fine = Mesh(mesh.devices.reshape(4, 2, 4, 4), ("z", "core", "y", "x"))
    row = P(EXPERT, None)
    wide = P(EXPERT, None, ("y", "x"))
    tall = P(EXPERT, ("y", "x"), None)
    return jax.shard_map(
        per_device,
        mesh=fine,
        in_specs=(row, row, row, row, wide, wide, tall),
        out_specs=(row, row),
        check_vma=False,
    )
```

```python
import jax
import jax.numpy as jnp
from jax import lax
from jax.experimental import pallas as pl
from jax.experimental.pallas import tpu as pltpu
from jax.sharding import Mesh
from jax.sharding import PartitionSpec as P

F32 = jnp.float32
BF16 = jnp.bfloat16
EXPERT = ("z", "core")
AXES = ("x", "y")
RING = 4
GROUPS = 8
ROWS = 256
MIB = 1 << 20


def shift(rows, axis, step):
    return lax.ppermute(rows, axis, [(i, (i + step) % RING) for i in range(RING)])


def dot(a, b):
    return jnp.dot(a, b, preferred_element_type=F32)


def dot_t(a, b):
    return lax.dot_general(a, b, (((1,), (1,)), ((), ())), preferred_element_type=F32)


def whole(shape):
    return pl.BlockSpec(shape, lambda *_: (0,) * len(shape))


def params(mib=58):
    return pltpu.CompilerParams(vmem_limit_bytes=mib * MIB)


def cost(flops, moved):
    return pl.CostEstimate(flops=int(flops), bytes_accessed=int(moved), transcendentals=0)


def slot_at(at, h):
    return (at >> 5) * 64 + h * 32 + (at & 31)


def dispatch_kernel(place, routes, *refs):
    columns, (placed, target) = refs[:2], refs[2:]
    tokens = routes.shape[0]
    row, lane = (lax.broadcasted_iota(jnp.int32, (tokens, tokens), d) for d in range(2))
    picks = [jnp.where(routes[:, k : k + 1] == lane, 1.0, 0.0) for k in range(2)]
    earlier = jnp.where(row > lane, 1.0, 0.0).astype(BF16)
    before = dot(earlier, (picks[0] + picks[1]).astype(BF16))
    targets = []
    for k in range(2):
        count = jnp.sum(picks[k] * before, axis=1, keepdims=True).astype(jnp.int32)
        targets.append(routes[:, k : k + 1] * (2 * ROWS // GROUPS) + count)
        target[:, k : k + 1] = targets[k]
    slot_lane = lax.broadcasted_iota(jnp.int32, (tokens, ROWS), 1)
    for h in range(2):
        slot = slot_at(slot_lane, h)
        chosen = jnp.where((targets[0] == slot) | (targets[1] == slot), 1.0, 0.0)
        rows = dot(chosen.T.astype(BF16), columns[h][...]).astype(BF16)
        placed[:, h] = rows.reshape(placed.shape[0], placed.shape[2], placed.shape[3])


def dispatch(place, routes, rows):
    tokens, width = rows.shape
    chunk = width // RING
    shape = (GROUPS, 2, ROWS // GROUPS, chunk)
    return pl.pallas_call(
        dispatch_kernel,
        out_shape=[jax.ShapeDtypeStruct(shape, BF16), jax.ShapeDtypeStruct(routes.shape, jnp.int32)],
        grid_spec=pltpu.PrefetchScalarGridSpec(
            num_scalar_prefetch=1,
            grid=(1,),
            in_specs=[whole(routes.shape)]
            + [pl.BlockSpec((tokens, chunk), lambda i, place, h=h: (0, place[h])) for h in range(2)],
            out_specs=[whole(shape), whole(routes.shape)],
        ),
        compiler_params=params(16),
        cost_estimate=cost(8 * ROWS * tokens * chunk, 8 * tokens * chunk + 4 * ROWS * chunk),
        name="dispatch",
    )(place, routes, rows, rows)


def halves_kernel(*refs):
    for source, to in zip(refs[:4], refs[4:]):
        to[...] = source[...]


def gathered(owns):
    rows, chunk = owns[0].shape
    half = rows // 2
    befores = [shift(own, axis, 1) for own, axis in zip(owns, AXES)]
    afters = [shift(own, axis, -1) for own, axis in zip(owns, AXES)]
    top = pl.BlockSpec((half, chunk), lambda i: (0, 0))
    bottom = pl.BlockSpec((half, chunk), lambda i: (1, 0))
    send = pl.pallas_call(
        halves_kernel,
        out_shape=[jax.ShapeDtypeStruct((half, chunk), BF16)] * 4,
        grid=(1,),
        in_specs=[top, top, bottom, bottom],
        out_specs=[whole((half, chunk))] * 4,
        compiler_params=params(),
        cost_estimate=cost(0, 16 * half * chunk),
        name="halves",
    )(*befores, *afters)
    near = [[owns[h], afters[h], befores[h]] for h in range(2)]
    far = [[shift(send[h], AXES[h], 1), shift(send[2 + h], AXES[h], -1)] for h in range(2)]
    return near, far


def forward_near_kernel(place, *refs):
    rows, (wg, wu), (gate, up) = refs[:6], refs[6:8], refs[8:]
    for h in range(2):
        for i in range(3):

            @pl.when((pl.program_id(0) == h) & (pl.program_id(1) == i))
            def _(h=h, i=i):
                block = rows[3 * h + i][...]
                for acc, w in ((gate, wg), (up, wu)):
                    value = dot(block, w[...])
                    acc[...] = value if i == 0 else acc[...] + value


def emit(at_step, distance, place, outs, product):
    part = outs[4].shape[-1]
    top, bottom = slice(0, ROWS // 2), slice(ROWS // 2, ROWS)
    for h in range(2):
        plus, minus, plus_later, minus_later, own = outs[5 * h : 5 * h + 5]
        chunk = (place[h] + distance) % RING
        columns = [
            pl.multiple_of((chunk * RING + j if h == 0 else j * RING + chunk) * part, part) for j in range(RING)
        ]
        values = product(h, columns).astype(BF16)
        for j in range(RING):
            value = values[:, j * part : (j + 1) * part]
            if at_step == 0:
                plus[0, j] = value[top]
                minus[0, j] = value[bottom]
            elif at_step == 1:
                plus_later[j] = value[top]
                plus[0, j] = value[bottom]
            elif at_step == 2:
                minus[0, j] = value[top]
                minus_later[j] = value[bottom]
            else:
                own[j] = value


def emitted(width, before, more):
    part = width // RING // RING
    half = (RING, ROWS // 2, part)
    shapes = [(2 + more, *half), (2 + more, *half), half, half, (RING, ROWS, part)]
    specs = [
        pl.BlockSpec((1, *half), lambda i, place: (jnp.clip(i - before, 0, 1), 0, 0, 0)),
        pl.BlockSpec((1, *half), lambda i, place: (jnp.clip(i - before - 1, 0, 1), 0, 0, 0)),
        whole(half),
        whole(half),
        whole((RING, ROWS, part)),
    ]
    return [jax.ShapeDtypeStruct(s, BF16) for s in shapes] * 2, specs * 2


DISTANCES = (2, 1, 3, 0)


def forward_far_kernel(place, *refs):
    rows, (wg, wu, gate, up, wd), (to_gate, to_up) = refs[:4], refs[4:9], refs[9:11]
    outs, (hidden, down, sem) = refs[11:21], refs[21:]
    step = pl.program_id(0)
    load = pltpu.make_async_copy(wd, down, sem)

    @pl.when(step == 0)
    def _():
        load.start()

    for h in range(2):

        @pl.when(step == h)
        def _(h=h):
            block = jnp.concatenate([rows[2 * h][...], rows[2 * h + 1][...]], axis=0)
            g = gate[...] + dot(block, wg[...])
            u = up[...] + dot(block, wu[...])
            s = 1.0 / (1.0 + jnp.exp(-g))
            hidden[h * ROWS : (h + 1) * ROWS] = (g * s * u).astype(BF16)
            to_gate[...] = u * s * (1.0 + g * (1.0 - s))
            to_up[...] = g * s

    @pl.when(step == 1)
    def _():
        load.wait()

    part = outs[4].shape[-1]

    def product(h, columns):
        weights = jnp.concatenate([down[:, pl.ds(at, part)] for at in columns], axis=1)
        return dot(hidden[h * ROWS : (h + 1) * ROWS], weights)

    for at_step, distance in enumerate(DISTANCES):

        @pl.when(step == 2 + at_step)
        def _(at_step=at_step, distance=distance):
            emit(at_step, distance, place, outs, product)


STEPS = 4


def backward_kernel(place, rows, wd, to_gate, to_up, wg, wu, *refs):
    outs, (acc, d_both, both, sems) = refs[:10], refs[10:]
    hid = wd.shape[0]
    step = pl.program_id(0)
    loads = [pltpu.make_async_copy(w, both.at[:, pl.ds(n * hid, hid)], sems.at[n]) for n, w in enumerate((wg, wu))]

    @pl.when(step == 0)
    def _():
        for load in loads:
            load.start()

    @pl.when(step < STEPS)
    def _():
        value = dot_t(jnp.concatenate([rows[:, h].reshape(ROWS, rows.shape[-1]) for h in range(2)], axis=0), wd[...])

        @pl.when(step == 0)
        def _():
            acc[...] = value

        @pl.when(step > 0)
        def _():
            acc[...] += value

    @pl.when(step == STEPS - 1)
    def _():
        d_both[:, :hid] = (acc[...] * to_gate[...]).astype(BF16)
        d_both[:, hid:] = (acc[...] * to_up[...]).astype(BF16)
        for load in loads:
            load.wait()

    part = outs[4].shape[-1]

    def product(h, columns):
        weights = jnp.concatenate([both[pl.ds(at, part)] for at in columns], axis=0)
        return dot_t(d_both[h * ROWS : (h + 1) * ROWS], weights)

    for at_step, distance in enumerate(DISTANCES):

        @pl.when(step == STEPS + at_step)
        def _(at_step=at_step, distance=distance):
            emit(at_step, distance, place, outs, product)


def forward(place, near, far, w_gate, w_up, w_down):
    width, hid = w_gate.shape
    chunk = width // RING

    def weights(distance):
        return pl.BlockSpec((chunk, hid), lambda *at: ((at[-1][at[0]] + distance(at)) % RING, 0))

    def by_half(*_):
        return pl.BlockSpec((ROWS, hid), lambda *at: (at[0], 0))

    near_w = weights(lambda at: jnp.where(at[1] == 2, 3, at[1]))
    rows = near[0] + near[1]
    gate, up = pl.pallas_call(
        forward_near_kernel,
        out_shape=[jax.ShapeDtypeStruct((2 * ROWS, hid), F32)] * 2,
        grid_spec=pltpu.PrefetchScalarGridSpec(
            num_scalar_prefetch=1,
            grid=(2, 3),
            in_specs=[whole(r.shape) for r in rows] + [near_w, near_w],
            out_specs=[by_half()] * 2,
        ),
        compiler_params=params(),
        cost_estimate=cost(6 * ROWS * width * hid, 3 * width * ROWS + 6 * width * hid),
        name="forward_near",
    )(place, *rows, w_gate, w_up)
    rows = far[0] + far[1]
    far_w = pl.BlockSpec((chunk, hid), lambda i, place: ((place[jnp.minimum(i, 1)] + 2) % RING, 0))
    half_rows = pl.BlockSpec((ROWS, hid), lambda i, place: (jnp.minimum(i, 1), 0))
    shapes, specs = emitted(width, 2, 0)
    outs = pl.pallas_call(
        forward_far_kernel,
        out_shape=[jax.ShapeDtypeStruct((2 * ROWS, hid), F32)] * 2 + shapes,
        grid_spec=pltpu.PrefetchScalarGridSpec(
            num_scalar_prefetch=1,
            grid=(6,),
            in_specs=[whole(r.shape) for r in rows]
            + [far_w, far_w, half_rows, half_rows, pl.BlockSpec(memory_space=pl.ANY)],
            out_specs=[half_rows] * 2 + specs,
            scratch_shapes=[
                pltpu.VMEM((2 * ROWS, hid), BF16),
                pltpu.VMEM((hid, width), BF16),
                pltpu.SemaphoreType.DMA,
            ],
        ),
        compiler_params=params(),
        cost_estimate=cost(6 * ROWS * width * hid, 2 * width * ROWS + 4 * width * hid + 16 * ROWS * hid),
        name="forward_far",
    )(place, *rows, w_gate, w_up, gate, up, w_down)
    return outs[0], outs[1], (outs[2:7], outs[7:])


def backward(place, rows, w_gate, w_up, w_down, to_gate, to_up):
    hid, width = w_down.shape
    count = 2 * ROWS
    block = width // STEPS
    rows = rows.reshape(GROUPS, 2, ROWS // GROUPS, width)
    shapes, specs = emitted(width, STEPS, 1)
    anywhere = pl.BlockSpec(memory_space=pl.ANY)
    outs = pl.pallas_call(
        backward_kernel,
        out_shape=shapes,
        grid_spec=pltpu.PrefetchScalarGridSpec(
            num_scalar_prefetch=1,
            grid=(STEPS + 4,),
            in_specs=[
                pl.BlockSpec((*rows.shape[:3], block), lambda i, place: (0, 0, 0, jnp.minimum(i, STEPS - 1))),
                pl.BlockSpec((hid, block), lambda i, place: (0, jnp.minimum(i, STEPS - 1))),
                whole((count, hid)),
                whole((count, hid)),
                anywhere,
                anywhere,
            ],
            out_specs=specs,
            scratch_shapes=[
                pltpu.VMEM((count, hid), F32),
                pltpu.VMEM((count, 2 * hid), BF16),
                pltpu.VMEM((width, 2 * hid), BF16),
                pltpu.SemaphoreType.DMA((2,)),
            ],
        ),
        compiler_params=params(),
        cost_estimate=cost(6 * count * width * hid, 4 * width * count + 6 * width * hid),
        name="backward",
    )(place, rows, w_down, to_gate, to_up, w_gate, w_up)
    return outs[:5], outs[5:]


def combine_kernel(target, weights, *refs):
    homes, mixed = refs[:-1], refs[-1]
    tokens, part = mixed.shape[2:]
    total = jnp.zeros((tokens, part), F32)
    for h, home in enumerate(homes):
        rows = home[:, 0].reshape(-1, part)
        slot = slot_at(lax.broadcasted_iota(jnp.int32, (tokens, rows.shape[0]), 1) & (ROWS - 1), h)
        for k in range(2):
            choose = jnp.where(target[:, k : k + 1] == slot, 1.0, 0.0).astype(BF16)
            total += weights[:, k : k + 1] * dot(choose, rows)
    for copy in range(mixed.shape[0]):
        mixed[copy, 0] = total.astype(BF16)


def combine(homes, target, weights, copies):
    tokens = target.shape[0]
    terms, _, slots, part = homes[0].shape
    return pl.pallas_call(
        combine_kernel,
        out_shape=jax.ShapeDtypeStruct((copies, 2, tokens, part), BF16),
        grid=(2,),
        in_specs=[whole(target.shape), whole(weights.shape)]
        + [pl.BlockSpec((terms, 1, slots, part), lambda n: (0, n, 0, 0)) for _ in homes],
        out_specs=pl.BlockSpec((copies, 1, tokens, part), lambda n: (0, n, 0, 0)),
        compiler_params=params(24),
        cost_estimate=cost(8 * tokens * homes[0].size, 4 * homes[0].size + 4 * copies * tokens * part),
        name="combine",
    )(target, weights, *homes)


def add(*terms):
    return sum(t.astype(F32) for t in terms).astype(BF16)


def later_kernel(*refs):
    for own, got, send in zip(refs[:4], refs[4:8], refs[-4:]):
        send[...] = add(own[...], got[0]).reshape(send.shape)


def total_kernel(*refs):
    half = ROWS // 2
    for n in range(2):
        for h in range(2):
            own, first_plus, first_minus, later_plus, later_minus = (r[...] for r in refs[10 * n + 5 * h : 10 * n + 5 * h + 5])
            own = own[0]
            first_plus, first_minus, later_plus, later_minus = (
                r.reshape(half, r.shape[-1]) for r in (first_plus, first_minus, later_plus, later_minus)
            )
            top = add(own[:half], later_plus, first_minus)
            bottom = add(own[half:], first_plus, later_minus)
            total = refs[20 + h]
            shape = (GROUPS // 2, *total.shape[3:])
            total[0, : GROUPS // 2, n] = top.reshape(shape)
            total[0, GROUPS // 2 :, n] = bottom.reshape(shape)


def both_ways(plus, minus):
    return [shift(p, axis, 1) for p, axis in zip(plus, AXES)] + [shift(m, axis, -1) for m, axis in zip(minus, AXES)]


def ring_join(parts, first, plus, minus):
    half = parts[0][2].shape
    block = pl.BlockSpec((1, *half), lambda i: (0, 0, 0, 0))
    third = pl.BlockSpec((1, *half), lambda i: (2, 0, 0, 0))
    buffers = [*plus, *minus]
    outs = pl.pallas_call(
        later_kernel,
        out_shape=[jax.ShapeDtypeStruct(b.shape, BF16) for b in buffers],
        grid=(1,),
        in_specs=[whole(half)] * 4 + [block] * 4 + [pl.BlockSpec(memory_space=pl.ANY)] * 4,
        out_specs=[third] * 4,
        input_output_aliases={8 + n: n for n in range(4)},
        compiler_params=params(),
        cost_estimate=cost(0, 24 * half[0] * half[1] * half[2]),
        name="ring_join",
    )(*[p[2] for p in parts], *[p[3] for p in parts], *first, *buffers)
    return outs[:2], outs[2:]


def ring_later(parts, first):
    half = parts[0][2].shape
    block = pl.BlockSpec((1, *half), lambda i: (0, 0, 0, 0))
    outs = pl.pallas_call(
        later_kernel,
        out_shape=[jax.ShapeDtypeStruct(half, BF16)] * 4,
        grid=(1,),
        in_specs=[whole(half)] * 4 + [block] * 4,
        out_specs=[whole(half)] * 4,
        compiler_params=params(),
        cost_estimate=cost(0, 24 * half[0] * half[1] * half[2]),
        name="ring_later",
    )(*[p[2] for p in parts], *[p[3] for p in parts], *first)
    return outs[:2], outs[2:]


def ring_end(out_parts, out_first, got, grad_parts, grad_later):
    _, rows, part = out_parts[0][4].shape
    own = pl.BlockSpec((1, rows, part), lambda j: (j, 0, 0))
    blocks = [pl.BlockSpec((1, 1, rows // 2, part), lambda j, n=n: (n, j, 0, 0)) for n in range(3)]
    later = pl.BlockSpec((1, rows // 2, part), lambda j: (j, 0, 0))
    operands, specs = [], []
    for h in range(2):
        operands += [out_parts[h][4], out_first[h], out_first[2 + h], got[h], got[2 + h]]
        specs += [own, blocks[1], blocks[1], blocks[2], blocks[2]]
    for h in range(2):
        operands += [grad_parts[h][4], got[h], got[2 + h], grad_later[h], grad_later[2 + h]]
        specs += [own, blocks[1], blocks[1], later, later]
    shape = (RING, GROUPS, 2, rows // GROUPS, part)
    return pl.pallas_call(
        total_kernel,
        out_shape=[jax.ShapeDtypeStruct(shape, BF16)] * 2,
        grid=(RING,),
        in_specs=specs,
        out_specs=[pl.BlockSpec((1, *shape[1:]), lambda j: (j, 0, 0, 0, 0))] * 2,
        compiler_params=params(),
        cost_estimate=cost(0, 32 * RING * rows * part),
        name="ring_end",
    )(*operands)


def assemble_kernel(slices, *results):
    count, _, _, part = slices.shape
    for n, result in enumerate(results):
        for c in range(count):
            result[:, c * part : (c + 1) * part] = slices[c, n]


def assemble(slices):
    count, _, tokens, part = slices.shape
    return pl.pallas_call(
        assemble_kernel,
        out_shape=[jax.ShapeDtypeStruct((tokens, count * part), BF16)] * 2,
        grid=(RING,),
        in_specs=[pl.BlockSpec((count // RING, 2, tokens, part), lambda i: (i, 0, 0, 0))],
        out_specs=[pl.BlockSpec((tokens, count // RING * part), lambda i: (0, i))] * 2,
        compiler_params=params(),
        cost_estimate=cost(0, 4 * slices.size),
        name="assemble",
    )(slices)


def per_device(tokens, routes, route_weights, out_grad, w_gate, w_up, w_down):
    count_rows, width = tokens.shape
    half = ROWS // GROUPS
    chunk = width // RING
    part = chunk // RING
    w_gate, w_up, w_down = w_gate[0], w_up[0], w_down[0]
    places = jnp.stack([lax.axis_index(axis) for axis in AXES]).astype(jnp.int32)

    def to_experts(rows):
        return lax.all_to_all(rows, EXPERT, split_axis=0, concat_axis=0, tiled=True)

    quarters, target = dispatch(places, routes, tokens)
    got = to_experts(quarters)
    every = jnp.arange(2 * ROWS, dtype=jnp.int32)[:, None]
    chosen = ((every == target[None, :, 0]) | (every == target[None, :, 1])).astype(BF16)
    rows_g = to_experts(dot(chosen, out_grad).astype(BF16))
    near, far = gathered([got[:, h].reshape(ROWS, chunk) for h in range(2)])
    to_gate, to_up, out_parts = forward(places, near, far, w_gate, w_up, w_down)
    out_first = both_ways([p[0] for p in out_parts], [p[1] for p in out_parts])
    grad_parts = backward(places, rows_g, w_gate, w_up, w_down, to_gate, to_up)
    plus, minus = ring_join(out_parts, out_first, [p[0] for p in grad_parts], [p[1] for p in grad_parts])
    got = both_ways(plus, minus)
    grad_later = both_ways(*ring_later(grad_parts, got))
    totals = ring_end(out_parts, out_first, got, grad_parts, grad_later)
    homes = []
    for h in range(2):
        pieces = totals[h].reshape(RING * GROUPS, 2, half, part)
        axes = (AXES[1 - h], *EXPERT)
        homes.append(lax.all_to_all(pieces, axes, split_axis=0, concat_axis=0, tiled=True))
    copies = combine(homes, target, route_weights, RING * RING)
    moe_out, input_grad = assemble(lax.all_to_all(copies, AXES, split_axis=0, concat_axis=0, tiled=True))
    return moe_out, input_grad


def solution(mesh):
    fine = Mesh(mesh.devices.reshape(4, 2, 4, 4), ("z", "core", "y", "x"))
    row = P(EXPERT, None)
    wide = P(EXPERT, None, ("y", "x"))
    tall = P(EXPERT, ("y", "x"), None)
    return jax.shard_map(
        per_device,
        mesh=fine,
        in_specs=(row, row, row, row, wide, wide, tall),
        out_specs=(row, row),
        check_vma=False,
    )
```

```python
import functools

import jax
import jax.numpy as jnp
from jax import lax
from jax.experimental import pallas as pl
from jax.experimental.pallas import tpu as pltpu
from jax.sharding import Mesh
from jax.sharding import PartitionSpec as P

F32 = jnp.float32
BF16 = jnp.bfloat16
EXPERT = ("z", "core")
AXES = ("x", "y")
RING = 4
GROUPS = 8
ROWS = 256
MIB = 1 << 20


def shift(rows, axis, step):
    return lax.ppermute(rows, axis, [(i, (i + step) % RING) for i in range(RING)])


def dot(a, b):
    return jnp.dot(a, b, preferred_element_type=F32)


def dot_t(a, b):
    return lax.dot_general(a, b, (((1,), (1,)), ((), ())), preferred_element_type=F32)


def whole(shape):
    return pl.BlockSpec(shape, lambda *_: (0,) * len(shape))


def params(mib=63):
    return pltpu.CompilerParams(vmem_limit_bytes=mib * MIB)


def cost(flops, moved):
    return pl.CostEstimate(flops=int(flops), bytes_accessed=int(moved), transcendentals=0)


def slot_at(at, h):
    return (at >> 5) * 64 + h * 32 + (at & 31)


def dispatch_kernel(place, routes, *refs):
    columns, (placed, target) = refs[:2], refs[2:]
    tokens = routes.shape[0]
    row, lane = (lax.broadcasted_iota(jnp.int32, (tokens, tokens), d) for d in range(2))
    picks = [jnp.where(routes[:, k : k + 1] == lane, 1.0, 0.0) for k in range(2)]
    earlier = jnp.where(row > lane, 1.0, 0.0).astype(BF16)
    before = dot(earlier, (picks[0] + picks[1]).astype(BF16))
    targets = []
    for k in range(2):
        count = jnp.sum(picks[k] * before, axis=1, keepdims=True).astype(jnp.int32)
        targets.append(routes[:, k : k + 1] * (2 * ROWS // GROUPS) + count)
        target[:, k : k + 1] = targets[k]
    slot_lane = lax.broadcasted_iota(jnp.int32, (tokens, ROWS), 1)
    for h in range(2):
        slot = slot_at(slot_lane, h)
        chosen = jnp.where((targets[0] == slot) | (targets[1] == slot), 1.0, 0.0)
        rows = dot(chosen.T.astype(BF16), columns[h][...]).astype(BF16)
        placed[:, h] = rows.reshape(placed.shape[0], placed.shape[2], placed.shape[3])


def dispatch(place, routes, rows):
    tokens, width = rows.shape
    chunk = width // RING
    shape = (GROUPS, 2, ROWS // GROUPS, chunk)
    return pl.pallas_call(
        dispatch_kernel,
        out_shape=[jax.ShapeDtypeStruct(shape, BF16), jax.ShapeDtypeStruct(routes.shape, jnp.int32)],
        grid_spec=pltpu.PrefetchScalarGridSpec(
            num_scalar_prefetch=1,
            grid=(1,),
            in_specs=[whole(routes.shape)]
            + [pl.BlockSpec((tokens, chunk), lambda i, place, h=h: (0, place[h])) for h in range(2)],
            out_specs=[whole(shape), whole(routes.shape)],
        ),
        compiler_params=params(),
        cost_estimate=cost(8 * ROWS * tokens * chunk, 8 * tokens * chunk + 4 * ROWS * chunk),
        name="dispatch",
    )(place, routes, rows, rows)


ANYWHERE = pl.BlockSpec(memory_space=pl.ANY)


def halves_kernel(*refs):
    sources, ends, sems = refs[:4], refs[4:8], refs[8]
    half = ends[0].shape[0]
    copies = [
        pltpu.make_async_copy(source.at[pl.ds(n // 2 * half, half)], end, sems.at[n])
        for n, (source, end) in enumerate(zip(sources, ends))
    ]
    for copy in copies:
        copy.start()
    for copy in copies:
        copy.wait()


def gathered(owns):
    rows, chunk = owns[0].shape
    half = rows // 2
    befores = [shift(own, axis, 1) for own, axis in zip(owns, AXES)]
    afters = [shift(own, axis, -1) for own, axis in zip(owns, AXES)]
    send = pl.pallas_call(
        halves_kernel,
        out_shape=[jax.ShapeDtypeStruct((half, chunk), BF16)] * 4,
        in_specs=[ANYWHERE] * 4,
        out_specs=[ANYWHERE] * 4,
        scratch_shapes=[pltpu.SemaphoreType.DMA((4,))],
        compiler_params=params(),
        cost_estimate=cost(0, 16 * half * chunk),
        name="halves",
    )(*befores, *afters)
    near = [[owns[h], afters[h], befores[h]] for h in range(2)]
    far = [[shift(send[h], AXES[h], 1), shift(send[2 + h], AXES[h], -1)] for h in range(2)]
    return near, far


def forward_near_kernel(place, *refs):
    rows, (wg, wu), (gate, up) = refs[:6], refs[6:8], refs[8:]
    for h in range(2):
        for i in range(3):

            @pl.when((pl.program_id(0) == h) & (pl.program_id(1) == i))
            def _(h=h, i=i):
                block = rows[3 * h + i][...]
                for acc, w in ((gate, wg), (up, wu)):
                    value = dot(block, w[...])
                    acc[...] = value if i == 0 else acc[...] + value


def emit(at_step, distance, place, outs, product):
    part = outs[4].shape[-1]
    top, bottom = slice(0, ROWS // 2), slice(ROWS // 2, ROWS)
    for h in range(2):
        plus, minus, plus_later, minus_later, own = outs[5 * h : 5 * h + 5]
        chunk = (place[h] + distance) % RING
        columns = [
            pl.multiple_of((chunk * RING + j if h == 0 else j * RING + chunk) * part, part) for j in range(RING)
        ]
        values = product(h, columns).astype(BF16)
        for j in range(RING):
            value = values[:, j * part : (j + 1) * part]
            if at_step == 0:
                plus[0, j] = value[top]
                minus[0, j] = value[bottom]
            elif at_step == 1:
                plus_later[j] = value[top]
                plus[0, j] = value[bottom]
            elif at_step == 2:
                minus[0, j] = value[top]
                minus_later[j] = value[bottom]
            else:
                own[j] = value


def emitted(width, before, more):
    part = width // RING // RING
    half = (RING, ROWS // 2, part)
    shapes = [(2 + more, *half), (2 + more, *half), half, half, (RING, ROWS, part)]
    specs = [
        pl.BlockSpec((1, *half), lambda i, place: (jnp.clip(i - before, 0, 1), 0, 0, 0)),
        pl.BlockSpec((1, *half), lambda i, place: (jnp.clip(i - before - 1, 0, 1), 0, 0, 0)),
        whole(half),
        whole(half),
        whole((RING, ROWS, part)),
    ]
    return [jax.ShapeDtypeStruct(s, BF16) for s in shapes] * 2, specs * 2


DISTANCES = (2, 1, 3, 0)


def forward_far_kernel(place, *refs):
    rows, (wg, wu, gate, up, wd), (to_gate, to_up) = refs[:4], refs[4:9], refs[9:11]
    outs, (hidden, down, sem) = refs[11:21], refs[21:]
    step = pl.program_id(0)
    load = pltpu.make_async_copy(wd, down, sem)

    @pl.when(step == 0)
    def _():
        load.start()

    for h in range(2):

        @pl.when(step == h)
        def _(h=h):
            block = jnp.concatenate([rows[2 * h][...], rows[2 * h + 1][...]], axis=0)
            g = gate[...] + dot(block, wg[...])
            u = up[...] + dot(block, wu[...])
            s = 1.0 / (1.0 + jnp.exp(-g))
            hidden[h * ROWS : (h + 1) * ROWS] = (g * s * u).astype(BF16)
            to_gate[...] = u * s * (1.0 + g * (1.0 - s))
            to_up[...] = g * s

    @pl.when(step == 1)
    def _():
        load.wait()

    part = outs[4].shape[-1]

    def product(h, columns):
        weights = jnp.concatenate([down[:, pl.ds(at, part)] for at in columns], axis=1)
        return dot(hidden[h * ROWS : (h + 1) * ROWS], weights)

    for at_step, distance in enumerate(DISTANCES):

        @pl.when(step == 2 + at_step)
        def _(at_step=at_step, distance=distance):
            emit(at_step, distance, place, outs, product)


STEPS = 4


def backward_kernel(place, rows, wd, to_gate, to_up, wg, wu, *refs):
    outs, (acc, d_both, both, sems) = refs[:10], refs[10:]
    hid = wd.shape[0]
    step = pl.program_id(0)
    loads = [pltpu.make_async_copy(w, both.at[:, pl.ds(n * hid, hid)], sems.at[n]) for n, w in enumerate((wg, wu))]

    @pl.when(step == 0)
    def _():
        for load in loads:
            load.start()

    @pl.when(step < STEPS)
    def _():
        value = dot_t(jnp.concatenate([rows[:, h].reshape(ROWS, rows.shape[-1]) for h in range(2)], axis=0), wd[...])

        @pl.when(step == 0)
        def _():
            acc[...] = value

        @pl.when(step > 0)
        def _():
            acc[...] += value

    @pl.when(step == STEPS - 1)
    def _():
        d_both[:, :hid] = (acc[...] * to_gate[...]).astype(BF16)
        d_both[:, hid:] = (acc[...] * to_up[...]).astype(BF16)
        for load in loads:
            load.wait()

    part = outs[4].shape[-1]

    def product(h, columns):
        weights = jnp.concatenate([both[pl.ds(at, part)] for at in columns], axis=0)
        return dot_t(d_both[h * ROWS : (h + 1) * ROWS], weights)

    for at_step, distance in enumerate(DISTANCES):

        @pl.when(step == STEPS + at_step)
        def _(at_step=at_step, distance=distance):
            emit(at_step, distance, place, outs, product)


def forward(place, near, far, w_gate, w_up, w_down):
    width, hid = w_gate.shape
    chunk = width // RING

    def weights(distance):
        return pl.BlockSpec((chunk, hid), lambda *at: ((at[-1][at[0]] + distance(at)) % RING, 0))

    def by_half(*_):
        return pl.BlockSpec((ROWS, hid), lambda *at: (at[0], 0))

    near_w = weights(lambda at: jnp.where(at[1] == 2, 3, at[1]))
    rows = near[0] + near[1]
    gate, up = pl.pallas_call(
        forward_near_kernel,
        out_shape=[jax.ShapeDtypeStruct((2 * ROWS, hid), F32)] * 2,
        grid_spec=pltpu.PrefetchScalarGridSpec(
            num_scalar_prefetch=1,
            grid=(2, 3),
            in_specs=[whole(r.shape) for r in rows] + [near_w, near_w],
            out_specs=[by_half()] * 2,
        ),
        compiler_params=params(),
        cost_estimate=cost(6 * ROWS * width * hid, 3 * width * ROWS + 6 * width * hid),
        name="forward_near",
    )(place, *rows, w_gate, w_up)
    rows = far[0] + far[1]
    far_w = pl.BlockSpec((chunk, hid), lambda i, place: ((place[jnp.minimum(i, 1)] + 2) % RING, 0))
    half_rows = pl.BlockSpec((ROWS, hid), lambda i, place: (jnp.minimum(i, 1), 0))
    shapes, specs = emitted(width, 2, 0)
    outs = pl.pallas_call(
        forward_far_kernel,
        out_shape=[jax.ShapeDtypeStruct((2 * ROWS, hid), F32)] * 2 + shapes,
        grid_spec=pltpu.PrefetchScalarGridSpec(
            num_scalar_prefetch=1,
            grid=(6,),
            in_specs=[whole(r.shape) for r in rows]
            + [far_w, far_w, half_rows, half_rows, pl.BlockSpec(memory_space=pl.ANY)],
            out_specs=[half_rows] * 2 + specs,
            scratch_shapes=[
                pltpu.VMEM((2 * ROWS, hid), BF16),
                pltpu.VMEM((hid, width), BF16),
                pltpu.SemaphoreType.DMA,
            ],
        ),
        compiler_params=params(),
        cost_estimate=cost(6 * ROWS * width * hid, 2 * width * ROWS + 4 * width * hid + 16 * ROWS * hid),
        name="forward_far",
    )(place, *rows, w_gate, w_up, gate, up, w_down)
    return outs[0], outs[1], (outs[2:7], outs[7:])


def backward(place, rows, w_gate, w_up, w_down, to_gate, to_up):
    hid, width = w_down.shape
    count = 2 * ROWS
    block = width // STEPS
    rows = rows.reshape(GROUPS, 2, ROWS // GROUPS, width)
    shapes, specs = emitted(width, STEPS, 1)
    outs = pl.pallas_call(
        backward_kernel,
        out_shape=shapes,
        grid_spec=pltpu.PrefetchScalarGridSpec(
            num_scalar_prefetch=1,
            grid=(STEPS + 4,),
            in_specs=[
                pl.BlockSpec((*rows.shape[:3], block), lambda i, place: (0, 0, 0, jnp.minimum(i, STEPS - 1))),
                pl.BlockSpec((hid, block), lambda i, place: (0, jnp.minimum(i, STEPS - 1))),
                whole((count, hid)),
                whole((count, hid)),
                ANYWHERE,
                ANYWHERE,
            ],
            out_specs=specs,
            scratch_shapes=[
                pltpu.VMEM((count, hid), F32),
                pltpu.VMEM((count, 2 * hid), BF16),
                pltpu.VMEM((width, 2 * hid), BF16),
                pltpu.SemaphoreType.DMA((2,)),
            ],
        ),
        compiler_params=params(),
        cost_estimate=cost(6 * count * width * hid, 4 * width * count + 6 * width * hid),
        name="backward",
    )(place, rows, w_down, to_gate, to_up, w_gate, w_up)
    return outs[:5], outs[5:]


def combine_kernel(target, weights, *refs):
    homes, mixed = refs[:-1], refs[-1]
    tokens, part = mixed.shape[2:]
    total = jnp.zeros((tokens, part), F32)
    for h, home in enumerate(homes):
        rows = home[:, 0].reshape(-1, part)
        slot = slot_at(lax.broadcasted_iota(jnp.int32, (tokens, rows.shape[0]), 1) & (ROWS - 1), h)
        for k in range(2):
            choose = jnp.where(target[:, k : k + 1] == slot, 1.0, 0.0).astype(BF16)
            total += weights[:, k : k + 1] * dot(choose, rows)
    for copy in range(mixed.shape[0]):
        mixed[copy, 0] = total.astype(BF16)


def combine(homes, target, weights, copies):
    tokens = target.shape[0]
    terms, _, slots, part = homes[0].shape
    return pl.pallas_call(
        combine_kernel,
        out_shape=jax.ShapeDtypeStruct((copies, 2, tokens, part), BF16),
        grid=(2,),
        in_specs=[whole(target.shape), whole(weights.shape)]
        + [pl.BlockSpec((terms, 1, slots, part), lambda n: (0, n, 0, 0)) for _ in homes],
        out_specs=pl.BlockSpec((copies, 1, tokens, part), lambda n: (0, n, 0, 0)),
        compiler_params=params(),
        cost_estimate=cost(8 * tokens * homes[0].size, 4 * homes[0].size + 4 * copies * tokens * part),
        name="combine",
    )(target, weights, *homes)


def add(*terms):
    return sum(t.astype(F32) for t in terms).astype(BF16)


def later_kernel(block, *refs):
    owns, gots, sends, (mine, came, in_sems, out_sems) = refs[:4], refs[4:8], refs[-8:-4], refs[-4:]
    loads, stores = [], []
    for n in range(4):
        loads.append(
            [
                pltpu.make_async_copy(owns[n], mine.at[n], in_sems.at[0, n]),
                pltpu.make_async_copy(gots[n].at[0], came.at[n], in_sems.at[1, n]),
            ]
        )
        to = sends[n] if block is None else sends[n].at[block]
        stores.append(pltpu.make_async_copy(mine.at[n], to, out_sems.at[n]))
        for load in loads[n]:
            load.start()
    for n in range(4):
        for load in loads[n]:
            load.wait()
        mine[n] = add(mine[n], came[n])
        stores[n].start()
    for store in stores:
        store.wait()


def later_scratch(half):
    return [pltpu.VMEM((4, *half), BF16)] * 2 + [pltpu.SemaphoreType.DMA((2, 4)), pltpu.SemaphoreType.DMA((4,))]


def total_kernel(*refs):
    half = ROWS // 2
    for n in range(2):
        for h in range(2):
            own, first_plus, first_minus, later_plus, later_minus = (r[...] for r in refs[10 * n + 5 * h : 10 * n + 5 * h + 5])
            own = own[0]
            first_plus, first_minus, later_plus, later_minus = (
                r.reshape(half, r.shape[-1]) for r in (first_plus, first_minus, later_plus, later_minus)
            )
            top = add(own[:half], later_plus, first_minus)
            bottom = add(own[half:], first_plus, later_minus)
            total = refs[20 + h]
            shape = (GROUPS // 2, *total.shape[3:])
            total[0, : GROUPS // 2, n] = top.reshape(shape)
            total[0, GROUPS // 2 :, n] = bottom.reshape(shape)


def both_ways(plus, minus):
    return [shift(p, axis, 1) for p, axis in zip(plus, AXES)] + [shift(m, axis, -1) for m, axis in zip(minus, AXES)]


def ring_join(parts, first, plus, minus):
    half = parts[0][2].shape
    buffers = [*plus, *minus]
    outs = pl.pallas_call(
        functools.partial(later_kernel, 2),
        out_shape=[jax.ShapeDtypeStruct(b.shape, BF16) for b in buffers],
        in_specs=[ANYWHERE] * 12,
        out_specs=[ANYWHERE] * 4,
        scratch_shapes=later_scratch(half),
        input_output_aliases={8 + n: n for n in range(4)},
        compiler_params=params(),
        cost_estimate=cost(0, 24 * half[0] * half[1] * half[2]),
        name="ring_join",
    )(*[p[2] for p in parts], *[p[3] for p in parts], *first, *buffers)
    return outs[:2], outs[2:]


def ring_later(parts, first):
    half = parts[0][2].shape
    outs = pl.pallas_call(
        functools.partial(later_kernel, None),
        out_shape=[jax.ShapeDtypeStruct(half, BF16)] * 4,
        in_specs=[ANYWHERE] * 8,
        out_specs=[ANYWHERE] * 4,
        scratch_shapes=later_scratch(half),
        compiler_params=params(),
        cost_estimate=cost(0, 24 * half[0] * half[1] * half[2]),
        name="ring_later",
    )(*[p[2] for p in parts], *[p[3] for p in parts], *first)
    return outs[:2], outs[2:]


def ring_end(out_parts, out_first, got, grad_parts, grad_later):
    _, rows, part = out_parts[0][4].shape
    own = pl.BlockSpec((1, rows, part), lambda j: (j, 0, 0))
    blocks = [pl.BlockSpec((1, 1, rows // 2, part), lambda j, n=n: (n, j, 0, 0)) for n in range(3)]
    later = pl.BlockSpec((1, rows // 2, part), lambda j: (j, 0, 0))
    operands, specs = [], []
    for h in range(2):
        operands += [out_parts[h][4], out_first[h], out_first[2 + h], got[h], got[2 + h]]
        specs += [own, blocks[1], blocks[1], blocks[2], blocks[2]]
    for h in range(2):
        operands += [grad_parts[h][4], got[h], got[2 + h], grad_later[h], grad_later[2 + h]]
        specs += [own, blocks[1], blocks[1], later, later]
    shape = (RING, GROUPS, 2, rows // GROUPS, part)
    return pl.pallas_call(
        total_kernel,
        out_shape=[jax.ShapeDtypeStruct(shape, BF16)] * 2,
        grid=(RING,),
        in_specs=specs,
        out_specs=[pl.BlockSpec((1, *shape[1:]), lambda j: (j, 0, 0, 0, 0))] * 2,
        compiler_params=params(),
        cost_estimate=cost(0, 32 * RING * rows * part),
        name="ring_end",
    )(*operands)


def assemble_kernel(slices, *refs):
    results, sems = refs[:2], refs[2]
    count, _, _, part = slices.shape
    copies = [
        pltpu.make_async_copy(slices.at[c, n], result.at[:, pl.ds(c * part, part)], sems.at[c, n])
        for c in range(count)
        for n, result in enumerate(results)
    ]
    for copy in copies:
        copy.start()
    for copy in copies:
        copy.wait()


def assemble(slices):
    count, _, tokens, part = slices.shape
    return pl.pallas_call(
        assemble_kernel,
        out_shape=[jax.ShapeDtypeStruct((tokens, count * part), BF16)] * 2,
        in_specs=[ANYWHERE],
        out_specs=[ANYWHERE] * 2,
        scratch_shapes=[pltpu.SemaphoreType.DMA((count, 2))],
        compiler_params=params(),
        cost_estimate=cost(0, 4 * slices.size),
        name="assemble",
    )(slices)


def per_device(tokens, routes, route_weights, out_grad, w_gate, w_up, w_down):
    count_rows, width = tokens.shape
    half = ROWS // GROUPS
    chunk = width // RING
    part = chunk // RING
    w_gate, w_up, w_down = w_gate[0], w_up[0], w_down[0]
    places = jnp.stack([lax.axis_index(axis) for axis in AXES]).astype(jnp.int32)

    def to_experts(rows):
        return lax.all_to_all(rows, EXPERT, split_axis=0, concat_axis=0, tiled=True)

    quarters, target = dispatch(places, routes, tokens)
    got = to_experts(quarters)
    every = jnp.arange(2 * ROWS, dtype=jnp.int32)[:, None]
    chosen = ((every == target[None, :, 0]) | (every == target[None, :, 1])).astype(BF16)
    rows_g = to_experts(dot(chosen, out_grad).astype(BF16))
    near, far = gathered([got[:, h].reshape(ROWS, chunk) for h in range(2)])
    to_gate, to_up, out_parts = forward(places, near, far, w_gate, w_up, w_down)
    out_first = both_ways([p[0] for p in out_parts], [p[1] for p in out_parts])
    grad_parts = backward(places, rows_g, w_gate, w_up, w_down, to_gate, to_up)
    plus, minus = ring_join(out_parts, out_first, [p[0] for p in grad_parts], [p[1] for p in grad_parts])
    got = both_ways(plus, minus)
    grad_later = both_ways(*ring_later(grad_parts, got))
    totals = ring_end(out_parts, out_first, got, grad_parts, grad_later)
    homes = []
    for h in range(2):
        pieces = totals[h].reshape(RING * GROUPS, 2, half, part)
        axes = (AXES[1 - h], *EXPERT)
        homes.append(lax.all_to_all(pieces, axes, split_axis=0, concat_axis=0, tiled=True))
    copies = combine(homes, target, route_weights, RING * RING)
    moe_out, input_grad = assemble(lax.all_to_all(copies, AXES, split_axis=0, concat_axis=0, tiled=True))
    return moe_out, input_grad


def solution(mesh):
    fine = Mesh(mesh.devices.reshape(4, 2, 4, 4), ("z", "core", "y", "x"))
    row = P(EXPERT, None)
    wide = P(EXPERT, None, ("y", "x"))
    tall = P(EXPERT, ("y", "x"), None)
    return jax.shard_map(
        per_device,
        mesh=fine,
        in_specs=(row, row, row, row, wide, wide, tall),
        out_specs=(row, row),
        check_vma=False,
    )
```

```python
import functools

import jax
import jax.numpy as jnp
from jax import lax
from jax.experimental import pallas as pl
from jax.experimental.pallas import tpu as pltpu
from jax.sharding import Mesh
from jax.sharding import PartitionSpec as P

F32 = jnp.float32
BF16 = jnp.bfloat16
EXPERT = ("z", "core")
AXES = ("x", "y")
RING = 4
GROUPS = 8
ROWS = 256
MIB = 1 << 20


def shift(rows, axis, step):
    return lax.ppermute(rows, axis, [(i, (i + step) % RING) for i in range(RING)])


def dot(a, b):
    return jnp.dot(a, b, preferred_element_type=F32)


def dot_t(a, b):
    return lax.dot_general(a, b, (((1,), (1,)), ((), ())), preferred_element_type=F32)


def whole(shape):
    return pl.BlockSpec(shape, lambda *_: (0,) * len(shape))


def params(mib=63):
    return pltpu.CompilerParams(vmem_limit_bytes=mib * MIB)


def cost(flops, moved):
    return pl.CostEstimate(flops=int(flops), bytes_accessed=int(moved), transcendentals=0)


def slot_at(at, h):
    return (at >> 5) * 64 + h * 32 + (at & 31)


def dispatch_kernel(place, routes, *refs):
    columns, (placed, target) = refs[:2], refs[2:]
    tokens = routes.shape[0]
    row, lane = (lax.broadcasted_iota(jnp.int32, (tokens, tokens), d) for d in range(2))
    picks = [jnp.where(routes[:, k : k + 1] == lane, 1.0, 0.0) for k in range(2)]
    earlier = jnp.where(row > lane, 1.0, 0.0).astype(BF16)
    before = dot(earlier, (picks[0] + picks[1]).astype(BF16))
    targets = []
    for k in range(2):
        count = jnp.sum(picks[k] * before, axis=1, keepdims=True).astype(jnp.int32)
        targets.append(routes[:, k : k + 1] * (2 * ROWS // GROUPS) + count)
        target[:, k : k + 1] = targets[k]
    slot_lane = lax.broadcasted_iota(jnp.int32, (tokens, ROWS), 1)
    for h in range(2):
        slot = slot_at(slot_lane, h)
        chosen = jnp.where((targets[0] == slot) | (targets[1] == slot), 1.0, 0.0)
        rows = dot(chosen.T.astype(BF16), columns[h][...]).astype(BF16)
        placed[:, h] = rows.reshape(placed.shape[0], placed.shape[2], placed.shape[3])


def dispatch(place, routes, rows):
    tokens, width = rows.shape
    chunk = width // RING
    shape = (GROUPS, 2, ROWS // GROUPS, chunk)
    return pl.pallas_call(
        dispatch_kernel,
        out_shape=[jax.ShapeDtypeStruct(shape, BF16), jax.ShapeDtypeStruct(routes.shape, jnp.int32)],
        grid_spec=pltpu.PrefetchScalarGridSpec(
            num_scalar_prefetch=1,
            grid=(1,),
            in_specs=[whole(routes.shape)]
            + [pl.BlockSpec((tokens, chunk), lambda i, place, h=h: (0, place[h])) for h in range(2)],
            out_specs=[whole(shape), whole(routes.shape)],
        ),
        compiler_params=params(16),
        cost_estimate=cost(8 * ROWS * tokens * chunk, 8 * tokens * chunk + 4 * ROWS * chunk),
        name="dispatch",
    )(place, routes, rows, rows)


ANYWHERE = pl.BlockSpec(memory_space=pl.ANY)


def halves_kernel(*refs):
    for source, to in zip(refs[:4], refs[4:]):
        to[...] = source[...]


def gathered(owns):
    rows, chunk = owns[0].shape
    half = rows // 2
    befores = [shift(own, axis, 1) for own, axis in zip(owns, AXES)]
    afters = [shift(own, axis, -1) for own, axis in zip(owns, AXES)]
    top = pl.BlockSpec((half, chunk), lambda i: (0, 0))
    bottom = pl.BlockSpec((half, chunk), lambda i: (1, 0))
    send = pl.pallas_call(
        halves_kernel,
        out_shape=[jax.ShapeDtypeStruct((half, chunk), BF16)] * 4,
        grid=(1,),
        in_specs=[top, top, bottom, bottom],
        out_specs=[whole((half, chunk))] * 4,
        compiler_params=params(58),
        cost_estimate=cost(0, 16 * half * chunk),
        name="halves",
    )(*befores, *afters)
    near = [[owns[h], afters[h], befores[h]] for h in range(2)]
    far = [[shift(send[h], AXES[h], 1), shift(send[2 + h], AXES[h], -1)] for h in range(2)]
    return near, far


def forward_near_kernel(place, *refs):
    rows, (wg, wu), (gate, up) = refs[:6], refs[6:8], refs[8:]
    for h in range(2):
        for i in range(3):

            @pl.when((pl.program_id(0) == h) & (pl.program_id(1) == i))
            def _(h=h, i=i):
                block = rows[3 * h + i][...]
                for acc, w in ((gate, wg), (up, wu)):
                    value = dot(block, w[...])
                    acc[...] = value if i == 0 else acc[...] + value


def emit(at_step, distance, place, outs, product):
    part = outs[4].shape[-1]
    top, bottom = slice(0, ROWS // 2), slice(ROWS // 2, ROWS)
    for h in range(2):
        plus, minus, plus_later, minus_later, own = outs[5 * h : 5 * h + 5]
        chunk = (place[h] + distance) % RING
        columns = [
            pl.multiple_of((chunk * RING + j if h == 0 else j * RING + chunk) * part, part) for j in range(RING)
        ]
        values = product(h, columns).astype(BF16)
        for j in range(RING):
            value = values[:, j * part : (j + 1) * part]
            if at_step == 0:
                plus[0, j] = value[top]
                minus[0, j] = value[bottom]
            elif at_step == 1:
                plus_later[j] = value[top]
                plus[0, j] = value[bottom]
            elif at_step == 2:
                minus[0, j] = value[top]
                minus_later[j] = value[bottom]
            else:
                own[j] = value


def emitted(width, before, more):
    part = width // RING // RING
    half = (RING, ROWS // 2, part)
    shapes = [(2 + more, *half), (2 + more, *half), half, half, (RING, ROWS, part)]
    specs = [
        pl.BlockSpec((1, *half), lambda i, place: (jnp.clip(i - before, 0, 1), 0, 0, 0)),
        pl.BlockSpec((1, *half), lambda i, place: (jnp.clip(i - before - 1, 0, 1), 0, 0, 0)),
        whole(half),
        whole(half),
        whole((RING, ROWS, part)),
    ]
    return [jax.ShapeDtypeStruct(s, BF16) for s in shapes] * 2, specs * 2


DISTANCES = (2, 1, 3, 0)


def forward_far_kernel(place, *refs):
    rows, (wg, wu, gate, up, wd), (to_gate, to_up) = refs[:4], refs[4:9], refs[9:11]
    outs, (hidden, down, sem) = refs[11:21], refs[21:]
    step = pl.program_id(0)
    load = pltpu.make_async_copy(wd, down, sem)

    @pl.when(step == 0)
    def _():
        load.start()

    for h in range(2):

        @pl.when(step == h)
        def _(h=h):
            block = jnp.concatenate([rows[2 * h][...], rows[2 * h + 1][...]], axis=0)
            g = gate[...] + dot(block, wg[...])
            u = up[...] + dot(block, wu[...])
            s = 1.0 / (1.0 + jnp.exp(-g))
            hidden[h * ROWS : (h + 1) * ROWS] = (g * s * u).astype(BF16)
            to_gate[...] = u * s * (1.0 + g * (1.0 - s))
            to_up[...] = g * s

    @pl.when(step == 1)
    def _():
        load.wait()

    part = outs[4].shape[-1]

    def product(h, columns):
        weights = jnp.concatenate([down[:, pl.ds(at, part)] for at in columns], axis=1)
        return dot(hidden[h * ROWS : (h + 1) * ROWS], weights)

    for at_step, distance in enumerate(DISTANCES):

        @pl.when(step == 2 + at_step)
        def _(at_step=at_step, distance=distance):
            emit(at_step, distance, place, outs, product)


STEPS = 2


def backward_kernel(place, rows, wd, to_gate, to_up, wg, wu, *refs):
    outs, (acc, d_both, both, sems) = refs[:10], refs[10:]
    hid = wd.shape[0]
    step = pl.program_id(0)
    loads = [pltpu.make_async_copy(w, both.at[:, pl.ds(n * hid, hid)], sems.at[n]) for n, w in enumerate((wg, wu))]

    @pl.when(step == 0)
    def _():
        for load in loads:
            load.start()

    @pl.when(step < STEPS)
    def _():
        value = dot_t(jnp.concatenate([rows[:, h].reshape(ROWS, rows.shape[-1]) for h in range(2)], axis=0), wd[...])

        @pl.when(step == 0)
        def _():
            acc[...] = value

        @pl.when(step > 0)
        def _():
            acc[...] += value

    @pl.when(step == STEPS - 1)
    def _():
        d_both[:, :hid] = (acc[...] * to_gate[...]).astype(BF16)
        d_both[:, hid:] = (acc[...] * to_up[...]).astype(BF16)
        for load in loads:
            load.wait()

    part = outs[4].shape[-1]

    def product(h, columns):
        weights = jnp.concatenate([both[pl.ds(at, part)] for at in columns], axis=0)
        return dot_t(d_both[h * ROWS : (h + 1) * ROWS], weights)

    for at_step, distance in enumerate(DISTANCES):

        @pl.when(step == STEPS + at_step)
        def _(at_step=at_step, distance=distance):
            emit(at_step, distance, place, outs, product)


def forward(place, near, far, w_gate, w_up, w_down):
    width, hid = w_gate.shape
    chunk = width // RING

    def weights(distance):
        return pl.BlockSpec((chunk, hid), lambda *at: ((at[-1][at[0]] + distance(at)) % RING, 0))

    def by_half(*_):
        return pl.BlockSpec((ROWS, hid), lambda *at: (at[0], 0))

    near_w = weights(lambda at: jnp.where(at[1] == 2, 3, at[1]))
    rows = near[0] + near[1]
    gate, up = pl.pallas_call(
        forward_near_kernel,
        out_shape=[jax.ShapeDtypeStruct((2 * ROWS, hid), F32)] * 2,
        grid_spec=pltpu.PrefetchScalarGridSpec(
            num_scalar_prefetch=1,
            grid=(2, 3),
            in_specs=[whole(r.shape) for r in rows] + [near_w, near_w],
            out_specs=[by_half()] * 2,
        ),
        compiler_params=params(63),
        cost_estimate=cost(6 * ROWS * width * hid, 3 * width * ROWS + 6 * width * hid),
        name="forward_near",
    )(place, *rows, w_gate, w_up)
    rows = far[0] + far[1]
    far_w = pl.BlockSpec((chunk, hid), lambda i, place: ((place[jnp.minimum(i, 1)] + 2) % RING, 0))
    half_rows = pl.BlockSpec((ROWS, hid), lambda i, place: (jnp.minimum(i, 1), 0))
    shapes, specs = emitted(width, 2, 0)
    outs = pl.pallas_call(
        forward_far_kernel,
        out_shape=[jax.ShapeDtypeStruct((2 * ROWS, hid), F32)] * 2 + shapes,
        grid_spec=pltpu.PrefetchScalarGridSpec(
            num_scalar_prefetch=1,
            grid=(6,),
            in_specs=[whole(r.shape) for r in rows]
            + [far_w, far_w, half_rows, half_rows, pl.BlockSpec(memory_space=pl.ANY)],
            out_specs=[half_rows] * 2 + specs,
            scratch_shapes=[
                pltpu.VMEM((2 * ROWS, hid), BF16),
                pltpu.VMEM((hid, width), BF16),
                pltpu.SemaphoreType.DMA,
            ],
        ),
        compiler_params=params(63),
        cost_estimate=cost(6 * ROWS * width * hid, 2 * width * ROWS + 4 * width * hid + 16 * ROWS * hid),
        name="forward_far",
    )(place, *rows, w_gate, w_up, gate, up, w_down)
    return outs[0], outs[1], (outs[2:7], outs[7:])


def backward(place, rows, w_gate, w_up, w_down, to_gate, to_up):
    hid, width = w_down.shape
    count = 2 * ROWS
    block = width // STEPS
    rows = rows.reshape(GROUPS, 2, ROWS // GROUPS, width)
    shapes, specs = emitted(width, STEPS, 1)
    outs = pl.pallas_call(
        backward_kernel,
        out_shape=shapes,
        grid_spec=pltpu.PrefetchScalarGridSpec(
            num_scalar_prefetch=1,
            grid=(STEPS + 4,),
            in_specs=[
                pl.BlockSpec((*rows.shape[:3], block), lambda i, place: (0, 0, 0, jnp.minimum(i, STEPS - 1))),
                pl.BlockSpec((hid, block), lambda i, place: (0, jnp.minimum(i, STEPS - 1))),
                whole((count, hid)),
                whole((count, hid)),
                ANYWHERE,
                ANYWHERE,
            ],
            out_specs=specs,
            scratch_shapes=[
                pltpu.VMEM((count, hid), F32),
                pltpu.VMEM((count, 2 * hid), BF16),
                pltpu.VMEM((width, 2 * hid), BF16),
                pltpu.SemaphoreType.DMA((2,)),
            ],
        ),
        compiler_params=params(),
        cost_estimate=cost(6 * count * width * hid, 4 * width * count + 6 * width * hid),
        name="backward",
    )(place, rows, w_down, to_gate, to_up, w_gate, w_up)
    return outs[:5], outs[5:]


def combine_kernel(target, weights, *refs):
    homes, mixed = refs[:-1], refs[-1]
    tokens, part = mixed.shape[2:]
    total = jnp.zeros((tokens, part), F32)
    for h, home in enumerate(homes):
        rows = home[:, 0].reshape(-1, part)
        slot = slot_at(lax.broadcasted_iota(jnp.int32, (tokens, rows.shape[0]), 1) & (ROWS - 1), h)
        for k in range(2):
            choose = jnp.where(target[:, k : k + 1] == slot, 1.0, 0.0).astype(BF16)
            total += weights[:, k : k + 1] * dot(choose, rows)
    for copy in range(mixed.shape[0]):
        mixed[copy, 0] = total.astype(BF16)


def combine(homes, target, weights, copies):
    tokens = target.shape[0]
    terms, _, slots, part = homes[0].shape
    return pl.pallas_call(
        combine_kernel,
        out_shape=jax.ShapeDtypeStruct((copies, 2, tokens, part), BF16),
        grid=(2,),
        in_specs=[whole(target.shape), whole(weights.shape)]
        + [pl.BlockSpec((terms, 1, slots, part), lambda n: (0, n, 0, 0)) for _ in homes],
        out_specs=pl.BlockSpec((copies, 1, tokens, part), lambda n: (0, n, 0, 0)),
        compiler_params=params(24),
        cost_estimate=cost(8 * tokens * homes[0].size, 4 * homes[0].size + 4 * copies * tokens * part),
        name="combine",
    )(target, weights, *homes)


def add(*terms):
    return sum(t.astype(F32) for t in terms).astype(BF16)


def later_kernel(block, *refs):
    owns, gots, sends, (mine, came, in_sems, out_sems) = refs[:4], refs[4:8], refs[-8:-4], refs[-4:]
    loads, stores = [], []
    for n in range(4):
        loads.append(
            [
                pltpu.make_async_copy(owns[n], mine.at[n], in_sems.at[0, n]),
                pltpu.make_async_copy(gots[n].at[0], came.at[n], in_sems.at[1, n]),
            ]
        )
        to = sends[n] if block is None else sends[n].at[block]
        stores.append(pltpu.make_async_copy(mine.at[n], to, out_sems.at[n]))
        for load in loads[n]:
            load.start()
    for n in range(4):
        for load in loads[n]:
            load.wait()
        mine[n] = add(mine[n], came[n])
        stores[n].start()
    for store in stores:
        store.wait()


def later_scratch(half):
    return [pltpu.VMEM((4, *half), BF16)] * 2 + [pltpu.SemaphoreType.DMA((2, 4)), pltpu.SemaphoreType.DMA((4,))]


def total_kernel(*refs):
    half = ROWS // 2
    for n in range(2):
        for h in range(2):
            own, first_plus, first_minus, later_plus, later_minus = (r[...] for r in refs[10 * n + 5 * h : 10 * n + 5 * h + 5])
            total = refs[20 + h]
            first_plus, first_minus, later_plus, later_minus = (
                r.reshape(-1, half, r.shape[-1]) for r in (first_plus, first_minus, later_plus, later_minus)
            )
            shape = (GROUPS // 2, *total.shape[3:])
            for j in range(own.shape[0]):
                top = add(own[j, :half], later_plus[j], first_minus[j])
                bottom = add(own[j, half:], first_plus[j], later_minus[j])
                total[j, : GROUPS // 2, n] = top.reshape(shape)
                total[j, GROUPS // 2 :, n] = bottom.reshape(shape)


def both_ways(plus, minus):
    return [shift(p, axis, 1) for p, axis in zip(plus, AXES)] + [shift(m, axis, -1) for m, axis in zip(minus, AXES)]


def ring_join(parts, first, plus, minus):
    half = parts[0][2].shape
    buffers = [*plus, *minus]
    outs = pl.pallas_call(
        functools.partial(later_kernel, 2),
        out_shape=[jax.ShapeDtypeStruct(b.shape, BF16) for b in buffers],
        in_specs=[ANYWHERE] * 12,
        out_specs=[ANYWHERE] * 4,
        scratch_shapes=later_scratch(half),
        input_output_aliases={8 + n: n for n in range(4)},
        compiler_params=params(),
        cost_estimate=cost(0, 24 * half[0] * half[1] * half[2]),
        name="ring_join",
    )(*[p[2] for p in parts], *[p[3] for p in parts], *first, *buffers)
    return outs[:2], outs[2:]


def ring_later(parts, first):
    half = parts[0][2].shape
    outs = pl.pallas_call(
        functools.partial(later_kernel, None),
        out_shape=[jax.ShapeDtypeStruct(half, BF16)] * 4,
        in_specs=[ANYWHERE] * 8,
        out_specs=[ANYWHERE] * 4,
        scratch_shapes=later_scratch(half),
        compiler_params=params(),
        cost_estimate=cost(0, 24 * half[0] * half[1] * half[2]),
        name="ring_later",
    )(*[p[2] for p in parts], *[p[3] for p in parts], *first)
    return outs[:2], outs[2:]


def ring_end(out_parts, out_first, got, grad_parts, grad_later):
    _, rows, part = out_parts[0][4].shape
    own = pl.BlockSpec((2, rows, part), lambda j: (j, 0, 0))
    blocks = [pl.BlockSpec((1, 2, rows // 2, part), lambda j, n=n: (n, j, 0, 0)) for n in range(3)]
    later = pl.BlockSpec((2, rows // 2, part), lambda j: (j, 0, 0))
    operands, specs = [], []
    for h in range(2):
        operands += [out_parts[h][4], out_first[h], out_first[2 + h], got[h], got[2 + h]]
        specs += [own, blocks[1], blocks[1], blocks[2], blocks[2]]
    for h in range(2):
        operands += [grad_parts[h][4], got[h], got[2 + h], grad_later[h], grad_later[2 + h]]
        specs += [own, blocks[1], blocks[1], later, later]
    shape = (RING, GROUPS, 2, rows // GROUPS, part)
    return pl.pallas_call(
        total_kernel,
        out_shape=[jax.ShapeDtypeStruct(shape, BF16)] * 2,
        grid=(2,),
        in_specs=specs,
        out_specs=[pl.BlockSpec((2, *shape[1:]), lambda j: (j, 0, 0, 0, 0))] * 2,
        compiler_params=params(),
        cost_estimate=cost(0, 32 * RING * rows * part),
        name="ring_end",
    )(*operands)


def assemble_kernel(slices, *results):
    count, _, _, part = slices.shape
    for n, result in enumerate(results):
        for c in range(count):
            result[:, c * part : (c + 1) * part] = slices[c, n]


def assemble(slices):
    count, _, tokens, part = slices.shape
    return pl.pallas_call(
        assemble_kernel,
        out_shape=[jax.ShapeDtypeStruct((tokens, count * part), BF16)] * 2,
        grid=(2,),
        in_specs=[pl.BlockSpec((count // 2, 2, tokens, part), lambda i: (i, 0, 0, 0))],
        out_specs=[pl.BlockSpec((tokens, count // 2 * part), lambda i: (0, i))] * 2,
        compiler_params=params(58),
        cost_estimate=cost(0, 4 * slices.size),
        name="assemble",
    )(slices)


def per_device(tokens, routes, route_weights, out_grad, w_gate, w_up, w_down):
    count_rows, width = tokens.shape
    half = ROWS // GROUPS
    chunk = width // RING
    part = chunk // RING
    w_gate, w_up, w_down = w_gate[0], w_up[0], w_down[0]
    places = jnp.stack([lax.axis_index(axis) for axis in AXES]).astype(jnp.int32)

    def to_experts(rows):
        return lax.all_to_all(rows, EXPERT, split_axis=0, concat_axis=0, tiled=True)

    quarters, target = dispatch(places, routes, tokens)
    got = to_experts(quarters)
    every = jnp.arange(2 * ROWS, dtype=jnp.int32)[:, None]
    chosen = ((every == target[None, :, 0]) | (every == target[None, :, 1])).astype(BF16)
    rows_g = to_experts(dot(chosen, out_grad).astype(BF16))
    near, far = gathered([got[:, h].reshape(ROWS, chunk) for h in range(2)])
    to_gate, to_up, out_parts = forward(places, near, far, w_gate, w_up, w_down)
    out_first = both_ways([p[0] for p in out_parts], [p[1] for p in out_parts])
    grad_parts = backward(places, rows_g, w_gate, w_up, w_down, to_gate, to_up)
    plus, minus = ring_join(out_parts, out_first, [p[0] for p in grad_parts], [p[1] for p in grad_parts])
    got = both_ways(plus, minus)
    grad_later = both_ways(*ring_later(grad_parts, got))
    totals = ring_end(out_parts, out_first, got, grad_parts, grad_later)
    homes = []
    for h in range(2):
        pieces = totals[h].reshape(RING * GROUPS, 2, half, part)
        axes = (AXES[1 - h], *EXPERT)
        homes.append(lax.all_to_all(pieces, axes, split_axis=0, concat_axis=0, tiled=True))
    copies = combine(homes, target, route_weights, RING * RING)
    moe_out, input_grad = assemble(lax.all_to_all(copies, AXES, split_axis=0, concat_axis=0, tiled=True))
    return moe_out, input_grad


def solution(mesh):
    fine = Mesh(mesh.devices.reshape(4, 2, 4, 4), ("z", "core", "y", "x"))
    row = P(EXPERT, None)
    wide = P(EXPERT, None, ("y", "x"))
    tall = P(EXPERT, ("y", "x"), None)
    return jax.shard_map(
        per_device,
        mesh=fine,
        in_specs=(row, row, row, row, wide, wide, tall),
        out_specs=(row, row),
        check_vma=False,
    )
```

```python
import functools

import jax
import jax.numpy as jnp
from jax import lax
from jax.experimental import pallas as pl
from jax.experimental.pallas import tpu as pltpu
from jax.sharding import Mesh
from jax.sharding import PartitionSpec as P

F32 = jnp.float32
BF16 = jnp.bfloat16
EXPERT = ("z", "core")
AXES = ("x", "y")
RING = 4
GROUPS = 8
ROWS = 256
MIB = 1 << 20


def shift(rows, axis, step):
    return lax.ppermute(rows, axis, [(i, (i + step) % RING) for i in range(RING)])


def dot(a, b):
    return jnp.dot(a, b, preferred_element_type=F32)


def dot_t(a, b):
    return lax.dot_general(a, b, (((1,), (1,)), ((), ())), preferred_element_type=F32)


def whole(shape):
    return pl.BlockSpec(shape, lambda *_: (0,) * len(shape))


def params(mib=63):
    return pltpu.CompilerParams(vmem_limit_bytes=mib * MIB)


def cost(flops, moved):
    return pl.CostEstimate(flops=int(flops), bytes_accessed=int(moved), transcendentals=0)


def slot_at(at, h):
    return (at >> 5) * 64 + h * 32 + (at & 31)


def dispatch_kernel(place, routes, *refs):
    columns, (placed, target) = refs[:2], refs[2:]
    tokens = routes.shape[0]
    row, lane = (lax.broadcasted_iota(jnp.int32, (tokens, tokens), d) for d in range(2))
    picks = [jnp.where(routes[:, k : k + 1] == lane, 1.0, 0.0) for k in range(2)]
    earlier = jnp.where(row > lane, 1.0, 0.0).astype(BF16)
    before = dot(earlier, (picks[0] + picks[1]).astype(BF16))
    targets = []
    for k in range(2):
        count = jnp.sum(picks[k] * before, axis=1, keepdims=True).astype(jnp.int32)
        targets.append(routes[:, k : k + 1] * (2 * ROWS // GROUPS) + count)
        target[:, k : k + 1] = targets[k]
    slot_lane = lax.broadcasted_iota(jnp.int32, (tokens, ROWS), 1)
    for h in range(2):
        slot = slot_at(slot_lane, h)
        chosen = jnp.where((targets[0] == slot) | (targets[1] == slot), 1.0, 0.0)
        rows = dot(chosen.T.astype(BF16), columns[h][...]).astype(BF16)
        placed[:, h] = rows.reshape(placed.shape[0], placed.shape[2], placed.shape[3])


def dispatch(place, routes, rows):
    tokens, width = rows.shape
    chunk = width // RING
    shape = (GROUPS, 2, ROWS // GROUPS, chunk)
    return pl.pallas_call(
        dispatch_kernel,
        out_shape=[jax.ShapeDtypeStruct(shape, BF16), jax.ShapeDtypeStruct(routes.shape, jnp.int32)],
        grid_spec=pltpu.PrefetchScalarGridSpec(
            num_scalar_prefetch=1,
            grid=(1,),
            in_specs=[whole(routes.shape)]
            + [pl.BlockSpec((tokens, chunk), lambda i, place, h=h: (0, place[h])) for h in range(2)],
            out_specs=[whole(shape), whole(routes.shape)],
        ),
        compiler_params=params(16),
        cost_estimate=cost(8 * ROWS * tokens * chunk, 8 * tokens * chunk + 4 * ROWS * chunk),
        name="dispatch",
    )(place, routes, rows, rows)


ANYWHERE = pl.BlockSpec(memory_space=pl.ANY)


def halves_kernel(*refs):
    for source, to in zip(refs[:4], refs[4:]):
        to[...] = source[...]


def gathered(owns):
    rows, chunk = owns[0].shape
    half = rows // 2
    befores = [shift(own, axis, 1) for own, axis in zip(owns, AXES)]
    afters = [shift(own, axis, -1) for own, axis in zip(owns, AXES)]
    top = pl.BlockSpec((half, chunk), lambda i: (0, 0))
    bottom = pl.BlockSpec((half, chunk), lambda i: (1, 0))
    send = pl.pallas_call(
        halves_kernel,
        out_shape=[jax.ShapeDtypeStruct((half, chunk), BF16)] * 4,
        grid=(1,),
        in_specs=[top, top, bottom, bottom],
        out_specs=[whole((half, chunk))] * 4,
        compiler_params=params(58),
        cost_estimate=cost(0, 16 * half * chunk),
        name="halves",
    )(*befores, *afters)
    near = [[owns[h], afters[h], befores[h]] for h in range(2)]
    far = [[shift(send[h], AXES[h], 1), shift(send[2 + h], AXES[h], -1)] for h in range(2)]
    return near, far


def forward_near_kernel(place, *refs):
    rows, (wg, wu), (gate, up) = refs[:6], refs[6:8], refs[8:]
    for h in range(2):
        for i in range(3):

            @pl.when((pl.program_id(0) == h) & (pl.program_id(1) == i))
            def _(h=h, i=i):
                block = rows[3 * h + i][...]
                for acc, w in ((gate, wg), (up, wu)):
                    value = dot(block, w[...])
                    acc[...] = value if i == 0 else acc[...] + value


def emit(at_step, distance, place, outs, product):
    part = outs[4].shape[-1]
    top, bottom = slice(0, ROWS // 2), slice(ROWS // 2, ROWS)
    for h in range(2):
        plus, minus, plus_later, minus_later, own = outs[5 * h : 5 * h + 5]
        chunk = (place[h] + distance) % RING
        columns = [
            pl.multiple_of((chunk * RING + j if h == 0 else j * RING + chunk) * part, part) for j in range(RING)
        ]
        values = product(h, columns).astype(BF16)
        for j in range(RING):
            value = values[:, j * part : (j + 1) * part]
            if at_step == 0:
                plus[0, j] = value[top]
                minus[0, j] = value[bottom]
            elif at_step == 1:
                plus_later[j] = value[top]
                plus[0, j] = value[bottom]
            elif at_step == 2:
                minus[0, j] = value[top]
                minus_later[j] = value[bottom]
            else:
                own[j] = value


def emitted(width, before, more):
    part = width // RING // RING
    half = (RING, ROWS // 2, part)
    shapes = [(2 + more, *half), (2 + more, *half), half, half, (RING, ROWS, part)]
    specs = [
        pl.BlockSpec((1, *half), lambda i, place: (jnp.clip(i - before, 0, 1), 0, 0, 0)),
        pl.BlockSpec((1, *half), lambda i, place: (jnp.clip(i - before - 1, 0, 1), 0, 0, 0)),
        whole(half),
        whole(half),
        whole((RING, ROWS, part)),
    ]
    return [jax.ShapeDtypeStruct(s, BF16) for s in shapes] * 2, specs * 2


DISTANCES = (2, 1, 3, 0)


def forward_far_kernel(place, *refs):
    rows, (wg, wu, gate, up, wd), (to_gate, to_up) = refs[:4], refs[4:9], refs[9:11]
    outs, (hidden, down, sem) = refs[11:21], refs[21:]
    step = pl.program_id(0)
    load = pltpu.make_async_copy(wd, down, sem)

    @pl.when(step == 0)
    def _():
        load.start()

    for h in range(2):

        @pl.when(step == h)
        def _(h=h):
            block = jnp.concatenate([rows[2 * h][...], rows[2 * h + 1][...]], axis=0)
            g = gate[...] + dot(block, wg[...])
            u = up[...] + dot(block, wu[...])
            s = 1.0 / (1.0 + jnp.exp(-g))
            hidden[h * ROWS : (h + 1) * ROWS] = (g * s * u).astype(BF16)
            to_gate[...] = u * s * (1.0 + g * (1.0 - s))
            to_up[...] = g * s

    @pl.when(step == 1)
    def _():
        load.wait()

    part = outs[4].shape[-1]

    def product(h, columns):
        weights = jnp.concatenate([down[:, pl.ds(at, part)] for at in columns], axis=1)
        return dot(hidden[h * ROWS : (h + 1) * ROWS], weights)

    for at_step, distance in enumerate(DISTANCES):

        @pl.when(step == 2 + at_step)
        def _(at_step=at_step, distance=distance):
            emit(at_step, distance, place, outs, product)


STEPS = 2


def backward_kernel(place, rows, wd, to_gate, to_up, wg, wu, *refs):
    outs, (acc, d_both, both, sems) = refs[:10], refs[10:]
    hid = wd.shape[0]
    step = pl.program_id(0)
    loads = [pltpu.make_async_copy(w, both.at[:, pl.ds(n * hid, hid)], sems.at[n]) for n, w in enumerate((wg, wu))]

    @pl.when(step == 0)
    def _():
        for load in loads:
            load.start()

    @pl.when(step < STEPS)
    def _():
        value = dot_t(jnp.concatenate([rows[:, h].reshape(ROWS, rows.shape[-1]) for h in range(2)], axis=0), wd[...])

        @pl.when(step == 0)
        def _():
            acc[...] = value

        @pl.when(step > 0)
        def _():
            acc[...] += value

    @pl.when(step == STEPS - 1)
    def _():
        d_both[:, :hid] = (acc[...] * to_gate[...]).astype(BF16)
        d_both[:, hid:] = (acc[...] * to_up[...]).astype(BF16)
        for load in loads:
            load.wait()

    part = outs[4].shape[-1]

    def product(h, columns):
        weights = jnp.concatenate([both[pl.ds(at, part)] for at in columns], axis=0)
        return dot_t(d_both[h * ROWS : (h + 1) * ROWS], weights)

    for at_step, distance in enumerate(DISTANCES):

        @pl.when(step == STEPS + at_step)
        def _(at_step=at_step, distance=distance):
            emit(at_step, distance, place, outs, product)


def forward(place, near, far, w_gate, w_up, w_down):
    width, hid = w_gate.shape
    chunk = width // RING

    def weights(distance):
        return pl.BlockSpec((chunk, hid), lambda *at: ((at[-1][at[0]] + distance(at)) % RING, 0))

    def by_half(*_):
        return pl.BlockSpec((ROWS, hid), lambda *at: (at[0], 0))

    near_w = weights(lambda at: jnp.where(at[1] == 2, 3, at[1]))
    rows = near[0] + near[1]
    gate, up = pl.pallas_call(
        forward_near_kernel,
        out_shape=[jax.ShapeDtypeStruct((2 * ROWS, hid), F32)] * 2,
        grid_spec=pltpu.PrefetchScalarGridSpec(
            num_scalar_prefetch=1,
            grid=(2, 3),
            in_specs=[whole(r.shape) for r in rows] + [near_w, near_w],
            out_specs=[by_half()] * 2,
        ),
        compiler_params=params(63),
        cost_estimate=cost(6 * ROWS * width * hid, 3 * width * ROWS + 6 * width * hid),
        name="forward_near",
    )(place, *rows, w_gate, w_up)
    rows = far[0] + far[1]
    far_w = pl.BlockSpec((chunk, hid), lambda i, place: ((place[jnp.minimum(i, 1)] + 2) % RING, 0))
    half_rows = pl.BlockSpec((ROWS, hid), lambda i, place: (jnp.minimum(i, 1), 0))
    shapes, specs = emitted(width, 2, 0)
    outs = pl.pallas_call(
        forward_far_kernel,
        out_shape=[jax.ShapeDtypeStruct((2 * ROWS, hid), F32)] * 2 + shapes,
        grid_spec=pltpu.PrefetchScalarGridSpec(
            num_scalar_prefetch=1,
            grid=(6,),
            in_specs=[whole(r.shape) for r in rows]
            + [far_w, far_w, half_rows, half_rows, pl.BlockSpec(memory_space=pl.ANY)],
            out_specs=[half_rows] * 2 + specs,
            scratch_shapes=[
                pltpu.VMEM((2 * ROWS, hid), BF16),
                pltpu.VMEM((hid, width), BF16),
                pltpu.SemaphoreType.DMA,
            ],
        ),
        compiler_params=params(63),
        cost_estimate=cost(6 * ROWS * width * hid, 2 * width * ROWS + 4 * width * hid + 16 * ROWS * hid),
        name="forward_far",
    )(place, *rows, w_gate, w_up, gate, up, w_down)
    return outs[0], outs[1], (outs[2:7], outs[7:])


def backward(place, rows, w_gate, w_up, w_down, to_gate, to_up):
    hid, width = w_down.shape
    count = 2 * ROWS
    block = width // STEPS
    rows = rows.reshape(GROUPS, 2, ROWS // GROUPS, width)
    shapes, specs = emitted(width, STEPS, 1)
    outs = pl.pallas_call(
        backward_kernel,
        out_shape=shapes,
        grid_spec=pltpu.PrefetchScalarGridSpec(
            num_scalar_prefetch=1,
            grid=(STEPS + 4,),
            in_specs=[
                pl.BlockSpec((*rows.shape[:3], block), lambda i, place: (0, 0, 0, jnp.minimum(i, STEPS - 1))),
                pl.BlockSpec((hid, block), lambda i, place: (0, jnp.minimum(i, STEPS - 1))),
                whole((count, hid)),
                whole((count, hid)),
                ANYWHERE,
                ANYWHERE,
            ],
            out_specs=specs,
            scratch_shapes=[
                pltpu.VMEM((count, hid), F32),
                pltpu.VMEM((count, 2 * hid), BF16),
                pltpu.VMEM((width, 2 * hid), BF16),
                pltpu.SemaphoreType.DMA((2,)),
            ],
        ),
        compiler_params=params(),
        cost_estimate=cost(6 * count * width * hid, 4 * width * count + 6 * width * hid),
        name="backward",
    )(place, rows, w_down, to_gate, to_up, w_gate, w_up)
    return outs[:5], outs[5:]


def combine_kernel(target, weights, *refs):
    homes, mixed = refs[:-1], refs[-1]
    tokens, part = mixed.shape[2:]
    total = jnp.zeros((tokens, part), F32)
    for h, home in enumerate(homes):
        rows = home[:, 0].reshape(-1, part)
        slot = slot_at(lax.broadcasted_iota(jnp.int32, (tokens, rows.shape[0]), 1) & (ROWS - 1), h)
        for k in range(2):
            choose = jnp.where(target[:, k : k + 1] == slot, 1.0, 0.0).astype(BF16)
            total += weights[:, k : k + 1] * dot(choose, rows)
    for copy in range(mixed.shape[0]):
        mixed[copy, 0] = total.astype(BF16)


def combine(homes, target, weights, copies):
    tokens = target.shape[0]
    terms, _, slots, part = homes[0].shape
    return pl.pallas_call(
        combine_kernel,
        out_shape=jax.ShapeDtypeStruct((copies, 2, tokens, part), BF16),
        grid=(2,),
        in_specs=[whole(target.shape), whole(weights.shape)]
        + [pl.BlockSpec((terms, 1, slots, part), lambda n: (0, n, 0, 0)) for _ in homes],
        out_specs=pl.BlockSpec((copies, 1, tokens, part), lambda n: (0, n, 0, 0)),
        compiler_params=params(24),
        cost_estimate=cost(8 * tokens * homes[0].size, 4 * homes[0].size + 4 * copies * tokens * part),
        name="combine",
    )(target, weights, *homes)


def add(*terms):
    return sum(t.astype(F32) for t in terms).astype(BF16)


def later_kernel(block, *refs):
    owns, gots, sends, (mine, came, in_sems, out_sems) = refs[:4], refs[4:8], refs[-8:-4], refs[-4:]
    loads, stores = [], []
    for n in range(4):
        loads.append(
            [
                pltpu.make_async_copy(owns[n], mine.at[n], in_sems.at[0, n]),
                pltpu.make_async_copy(gots[n].at[0], came.at[n], in_sems.at[1, n]),
            ]
        )
        to = sends[n] if block is None else sends[n].at[block]
        stores.append(pltpu.make_async_copy(mine.at[n], to, out_sems.at[n]))
        for load in loads[n]:
            load.start()
    for n in range(4):
        for load in loads[n]:
            load.wait()
        mine[n] = add(mine[n], came[n])
        stores[n].start()
    for store in stores:
        store.wait()


def later_scratch(half):
    return [pltpu.VMEM((4, *half), BF16)] * 2 + [pltpu.SemaphoreType.DMA((2, 4)), pltpu.SemaphoreType.DMA((4,))]


def total_kernel(*refs):
    half = ROWS // 2
    for h in range(2):
        own, first_plus, first_minus, later_plus, later_minus = (r[...] for r in refs[5 * h : 5 * h + 5])
        total = refs[-2 + h]
        first_plus, first_minus, later_plus, later_minus = (
            r.reshape(-1, half, r.shape[-1]) for r in (first_plus, first_minus, later_plus, later_minus)
        )
        shape = (GROUPS // 2, *total.shape[3:])
        for j in range(own.shape[0]):
            top = add(own[j, :half], later_plus[j], first_minus[j])
            bottom = add(own[j, half:], first_plus[j], later_minus[j])
            total[j, : GROUPS // 2, 0] = top.reshape(shape)
            total[j, GROUPS // 2 :, 0] = bottom.reshape(shape)


def both_ways(plus, minus):
    return [shift(p, axis, 1) for p, axis in zip(plus, AXES)] + [shift(m, axis, -1) for m, axis in zip(minus, AXES)]


def ring_join(parts, first, plus, minus):
    half = parts[0][2].shape
    buffers = [*plus, *minus]
    outs = pl.pallas_call(
        functools.partial(later_kernel, 2),
        out_shape=[jax.ShapeDtypeStruct(b.shape, BF16) for b in buffers],
        in_specs=[ANYWHERE] * 12,
        out_specs=[ANYWHERE] * 4,
        scratch_shapes=later_scratch(half),
        input_output_aliases={8 + n: n for n in range(4)},
        compiler_params=params(),
        cost_estimate=cost(0, 24 * half[0] * half[1] * half[2]),
        name="ring_join",
    )(*[p[2] for p in parts], *[p[3] for p in parts], *first, *buffers)
    return outs[:2], outs[2:]


def ring_later(parts, first):
    half = parts[0][2].shape
    outs = pl.pallas_call(
        functools.partial(later_kernel, None),
        out_shape=[jax.ShapeDtypeStruct(half, BF16)] * 4,
        in_specs=[ANYWHERE] * 8,
        out_specs=[ANYWHERE] * 4,
        scratch_shapes=later_scratch(half),
        compiler_params=params(),
        cost_estimate=cost(0, 24 * half[0] * half[1] * half[2]),
        name="ring_later",
    )(*[p[2] for p in parts], *[p[3] for p in parts], *first)
    return outs[:2], outs[2:]


def ring_end(parts, first, later, totals):
    _, rows, part = parts[0][4].shape
    own = pl.BlockSpec((2, rows, part), lambda j: (j, 0, 0))
    blocks = [pl.BlockSpec((1, 2, rows // 2, part), lambda j, n=n: (n, j, 0, 0)) for n in range(3)]
    last = blocks[2] if totals is None else pl.BlockSpec((2, rows // 2, part), lambda j: (j, 0, 0))
    operands, specs = [], []
    for h in range(2):
        operands += [parts[h][4], first[h], first[2 + h], later[h], later[2 + h]]
        specs += [own, blocks[1], blocks[1], last, last]
    number = 0 if totals is None else 1
    shape = (RING, GROUPS, 2, rows // GROUPS, part)
    return pl.pallas_call(
        total_kernel,
        out_shape=[jax.ShapeDtypeStruct(shape, BF16)] * 2,
        grid=(2,),
        in_specs=specs + [ANYWHERE] * (2 * number),
        out_specs=[pl.BlockSpec((2, GROUPS, 1, *shape[3:]), lambda j: (j, 0, number, 0, 0))] * 2,
        input_output_aliases={10 + h: h for h in range(2 * number)},
        compiler_params=params(),
        cost_estimate=cost(0, 16 * RING * rows * part),
        name="ring_end",
    )(*operands, *(totals or ()))


def assemble_kernel(slices, *results):
    count, _, _, part = slices.shape
    for n, result in enumerate(results):
        for c in range(count):
            result[:, c * part : (c + 1) * part] = slices[c, n]


def assemble(slices):
    count, _, tokens, part = slices.shape
    return pl.pallas_call(
        assemble_kernel,
        out_shape=[jax.ShapeDtypeStruct((tokens, count * part), BF16)] * 2,
        grid=(2,),
        in_specs=[pl.BlockSpec((count // 2, 2, tokens, part), lambda i: (i, 0, 0, 0))],
        out_specs=[pl.BlockSpec((tokens, count // 2 * part), lambda i: (0, i))] * 2,
        compiler_params=params(58),
        cost_estimate=cost(0, 4 * slices.size),
        name="assemble",
    )(slices)


def per_device(tokens, routes, route_weights, out_grad, w_gate, w_up, w_down):
    count_rows, width = tokens.shape
    half = ROWS // GROUPS
    chunk = width // RING
    part = chunk // RING
    w_gate, w_up, w_down = w_gate[0], w_up[0], w_down[0]
    places = jnp.stack([lax.axis_index(axis) for axis in AXES]).astype(jnp.int32)

    def to_experts(rows):
        return lax.all_to_all(rows, EXPERT, split_axis=0, concat_axis=0, tiled=True)

    quarters, target = dispatch(places, routes, tokens)
    got = to_experts(quarters)
    every = jnp.arange(2 * ROWS, dtype=jnp.int32)[:, None]
    chosen = ((every == target[None, :, 0]) | (every == target[None, :, 1])).astype(BF16)
    rows_g = to_experts(dot(chosen, out_grad).astype(BF16))
    near, far = gathered([got[:, h].reshape(ROWS, chunk) for h in range(2)])
    to_gate, to_up, out_parts = forward(places, near, far, w_gate, w_up, w_down)
    out_first = both_ways([p[0] for p in out_parts], [p[1] for p in out_parts])
    grad_parts = backward(places, rows_g, w_gate, w_up, w_down, to_gate, to_up)
    plus, minus = ring_join(out_parts, out_first, [p[0] for p in grad_parts], [p[1] for p in grad_parts])
    got = both_ways(plus, minus)
    grad_later = both_ways(*ring_later(grad_parts, got))
    totals = ring_end(out_parts, out_first, got, None)
    totals = ring_end(grad_parts, got, grad_later, totals)
    homes = []
    for h in range(2):
        pieces = totals[h].reshape(RING * GROUPS, 2, half, part)
        axes = (AXES[1 - h], *EXPERT)
        homes.append(lax.all_to_all(pieces, axes, split_axis=0, concat_axis=0, tiled=True))
    copies = combine(homes, target, route_weights, RING * RING)
    moe_out, input_grad = assemble(lax.all_to_all(copies, AXES, split_axis=0, concat_axis=0, tiled=True))
    return moe_out, input_grad


def solution(mesh):
    fine = Mesh(mesh.devices.reshape(4, 2, 4, 4), ("z", "core", "y", "x"))
    row = P(EXPERT, None)
    wide = P(EXPERT, None, ("y", "x"))
    tall = P(EXPERT, ("y", "x"), None)
    return jax.shard_map(
        per_device,
        mesh=fine,
        in_specs=(row, row, row, row, wide, wide, tall),
        out_specs=(row, row),
        check_vma=False,
    )
```

```python
import functools

import jax
import jax.numpy as jnp
from jax import lax
from jax.experimental import pallas as pl
from jax.experimental.pallas import tpu as pltpu
from jax.sharding import Mesh
from jax.sharding import PartitionSpec as P

F32 = jnp.float32
BF16 = jnp.bfloat16
EXPERT = ("z", "core")
AXES = ("x", "y")
RING = 4
GROUPS = 8
ROWS = 256
MIB = 1 << 20


def shift(rows, axis, step):
    return lax.ppermute(rows, axis, [(i, (i + step) % RING) for i in range(RING)])


def dot(a, b):
    return jnp.dot(a, b, preferred_element_type=F32)


def dot_t(a, b):
    return lax.dot_general(a, b, (((1,), (1,)), ((), ())), preferred_element_type=F32)


def whole(shape):
    return pl.BlockSpec(shape, lambda *_: (0,) * len(shape))


def params(mib=63):
    return pltpu.CompilerParams(vmem_limit_bytes=mib * MIB)


def cost(flops, moved):
    return pl.CostEstimate(flops=int(flops), bytes_accessed=int(moved), transcendentals=0)


def slot_at(at, h):
    return (at >> 5) * 64 + h * 32 + (at & 31)


def dispatch_kernel(place, routes, *refs):
    columns, (placed, target) = refs[:2], refs[2:]
    tokens = routes.shape[0]
    row, lane = (lax.broadcasted_iota(jnp.int32, (tokens, tokens), d) for d in range(2))
    picks = [jnp.where(routes[:, k : k + 1] == lane, 1.0, 0.0) for k in range(2)]
    earlier = jnp.where(row > lane, 1.0, 0.0).astype(BF16)
    before = dot(earlier, (picks[0] + picks[1]).astype(BF16))
    targets = []
    for k in range(2):
        count = jnp.sum(picks[k] * before, axis=1, keepdims=True).astype(jnp.int32)
        targets.append(routes[:, k : k + 1] * (2 * ROWS // GROUPS) + count)
        target[:, k : k + 1] = targets[k]
    slot_lane = lax.broadcasted_iota(jnp.int32, (tokens, ROWS), 1)
    for h in range(2):
        slot = slot_at(slot_lane, h)
        chosen = jnp.where((targets[0] == slot) | (targets[1] == slot), 1.0, 0.0)
        rows = dot(chosen.T.astype(BF16), columns[h][...]).astype(BF16)
        placed[:, h] = rows.reshape(placed.shape[0], placed.shape[2], placed.shape[3])


def dispatch(place, routes, rows):
    tokens, width = rows.shape
    chunk = width // RING
    shape = (GROUPS, 2, ROWS // GROUPS, chunk)
    return pl.pallas_call(
        dispatch_kernel,
        out_shape=[jax.ShapeDtypeStruct(shape, BF16), jax.ShapeDtypeStruct(routes.shape, jnp.int32)],
        grid_spec=pltpu.PrefetchScalarGridSpec(
            num_scalar_prefetch=1,
            grid=(1,),
            in_specs=[whole(routes.shape)]
            + [pl.BlockSpec((tokens, chunk), lambda i, place, h=h: (0, place[h])) for h in range(2)],
            out_specs=[whole(shape), whole(routes.shape)],
        ),
        compiler_params=params(16),
        cost_estimate=cost(8 * ROWS * tokens * chunk, 8 * tokens * chunk + 4 * ROWS * chunk),
        name="dispatch",
    )(place, routes, rows, rows)


ANYWHERE = pl.BlockSpec(memory_space=pl.ANY)


def halves_kernel(*refs):
    for source, to in zip(refs[:4], refs[4:]):
        to[...] = source[...]


def gathered(owns):
    rows, chunk = owns[0].shape
    half = rows // 2
    befores = [shift(own, axis, 1) for own, axis in zip(owns, AXES)]
    afters = [shift(own, axis, -1) for own, axis in zip(owns, AXES)]
    top = pl.BlockSpec((half, chunk), lambda i: (0, 0))
    bottom = pl.BlockSpec((half, chunk), lambda i: (1, 0))
    send = pl.pallas_call(
        halves_kernel,
        out_shape=[jax.ShapeDtypeStruct((half, chunk), BF16)] * 4,
        grid=(1,),
        in_specs=[top, top, bottom, bottom],
        out_specs=[whole((half, chunk))] * 4,
        compiler_params=params(58),
        cost_estimate=cost(0, 16 * half * chunk),
        name="halves",
    )(*befores, *afters)
    near = [[owns[h], afters[h], befores[h]] for h in range(2)]
    far = [[shift(send[h], AXES[h], 1), shift(send[2 + h], AXES[h], -1)] for h in range(2)]
    return near, far


def forward_near_kernel(place, *refs):
    rows, (wg, wu), (gate, up) = refs[:6], refs[6:8], refs[8:]
    for h in range(2):
        for i in range(3):

            @pl.when((pl.program_id(0) == h) & (pl.program_id(1) == i))
            def _(h=h, i=i):
                block = rows[3 * h + i][...]
                for acc, w in ((gate, wg), (up, wu)):
                    value = dot(block, w[...])
                    acc[...] = value if i == 0 else acc[...] + value


def emit(at_step, distance, place, outs, product):
    part = outs[4].shape[-1]
    top, bottom = slice(0, ROWS // 2), slice(ROWS // 2, ROWS)
    for h in range(2):
        plus, minus, plus_later, minus_later, own = outs[5 * h : 5 * h + 5]
        chunk = (place[h] + distance) % RING
        columns = [
            pl.multiple_of((chunk * RING + j if h == 0 else j * RING + chunk) * part, part) for j in range(RING)
        ]
        values = product(h, columns).astype(BF16)
        for j in range(RING):
            value = values[:, j * part : (j + 1) * part]
            if at_step == 0:
                plus[0, j] = value[top]
                minus[0, j] = value[bottom]
            elif at_step == 1:
                plus_later[j] = value[top]
                plus[0, j] = value[bottom]
            elif at_step == 2:
                minus[0, j] = value[top]
                minus_later[j] = value[bottom]
            else:
                own[j] = value


def emitted(width, before, more):
    part = width // RING // RING
    half = (RING, ROWS // 2, part)
    shapes = [(2 + more, *half), (2 + more, *half), half, half, (RING, ROWS, part)]
    specs = [
        pl.BlockSpec((1, *half), lambda i, place: (jnp.clip(i - before, 0, 1), 0, 0, 0)),
        pl.BlockSpec((1, *half), lambda i, place: (jnp.clip(i - before - 1, 0, 1), 0, 0, 0)),
        whole(half),
        whole(half),
        whole((RING, ROWS, part)),
    ]
    return [jax.ShapeDtypeStruct(s, BF16) for s in shapes] * 2, specs * 2


DISTANCES = (2, 1, 3, 0)


def forward_far_kernel(place, *refs):
    rows, (wg, wu, gate, up, wd), (to_gate, to_up) = refs[:4], refs[4:9], refs[9:11]
    outs, (hidden, down, sem) = refs[11:21], refs[21:]
    step = pl.program_id(0)
    load = pltpu.make_async_copy(wd, down, sem)

    @pl.when(step == 0)
    def _():
        load.start()

    for h in range(2):

        @pl.when(step == h)
        def _(h=h):
            block = jnp.concatenate([rows[2 * h][...], rows[2 * h + 1][...]], axis=0)
            g = gate[...] + dot(block, wg[...])
            u = up[...] + dot(block, wu[...])
            s = 1.0 / (1.0 + jnp.exp(-g))
            hidden[h * ROWS : (h + 1) * ROWS] = (g * s * u).astype(BF16)
            to_gate[...] = u * s * (1.0 + g * (1.0 - s))
            to_up[...] = g * s

    @pl.when(step == 1)
    def _():
        load.wait()

    part = outs[4].shape[-1]

    def product(h, columns):
        weights = jnp.concatenate([down[:, pl.ds(at, part)] for at in columns], axis=1)
        return dot(hidden[h * ROWS : (h + 1) * ROWS], weights)

    for at_step, distance in enumerate(DISTANCES):

        @pl.when(step == 2 + at_step)
        def _(at_step=at_step, distance=distance):
            emit(at_step, distance, place, outs, product)


STEPS = 2


def backward_kernel(place, rows, wd, to_gate, to_up, wg, wu, *refs):
    outs, (acc, d_both, both, sems) = refs[:10], refs[10:]
    hid = wd.shape[0]
    step = pl.program_id(0)
    loads = [pltpu.make_async_copy(w, both.at[:, pl.ds(n * hid, hid)], sems.at[n]) for n, w in enumerate((wg, wu))]

    @pl.when(step == 0)
    def _():
        for load in loads:
            load.start()

    @pl.when(step < STEPS)
    def _():
        value = dot_t(jnp.concatenate([rows[:, h].reshape(ROWS, rows.shape[-1]) for h in range(2)], axis=0), wd[...])

        @pl.when(step == 0)
        def _():
            acc[...] = value

        @pl.when(step > 0)
        def _():
            acc[...] += value

    @pl.when(step == STEPS - 1)
    def _():
        d_both[:, :hid] = (acc[...] * to_gate[...]).astype(BF16)
        d_both[:, hid:] = (acc[...] * to_up[...]).astype(BF16)
        for load in loads:
            load.wait()

    part = outs[4].shape[-1]

    def product(h, columns):
        weights = jnp.concatenate([both[pl.ds(at, part)] for at in columns], axis=0)
        return dot_t(d_both[h * ROWS : (h + 1) * ROWS], weights)

    for at_step, distance in enumerate(DISTANCES):

        @pl.when(step == STEPS + at_step)
        def _(at_step=at_step, distance=distance):
            emit(at_step, distance, place, outs, product)


def forward(place, near, far, w_gate, w_up, w_down):
    width, hid = w_gate.shape
    chunk = width // RING

    def weights(distance):
        return pl.BlockSpec((chunk, hid), lambda *at: ((at[-1][at[0]] + distance(at)) % RING, 0))

    def by_half(*_):
        return pl.BlockSpec((ROWS, hid), lambda *at: (at[0], 0))

    near_w = weights(lambda at: jnp.where(at[1] == 2, 3, at[1]))
    rows = near[0] + near[1]
    gate, up = pl.pallas_call(
        forward_near_kernel,
        out_shape=[jax.ShapeDtypeStruct((2 * ROWS, hid), F32)] * 2,
        grid_spec=pltpu.PrefetchScalarGridSpec(
            num_scalar_prefetch=1,
            grid=(2, 3),
            in_specs=[whole(r.shape) for r in rows] + [near_w, near_w],
            out_specs=[by_half()] * 2,
        ),
        compiler_params=params(63),
        cost_estimate=cost(6 * ROWS * width * hid, 3 * width * ROWS + 6 * width * hid),
        name="forward_near",
    )(place, *rows, w_gate, w_up)
    rows = far[0] + far[1]
    far_w = pl.BlockSpec((chunk, hid), lambda i, place: ((place[jnp.minimum(i, 1)] + 2) % RING, 0))
    half_rows = pl.BlockSpec((ROWS, hid), lambda i, place: (jnp.minimum(i, 1), 0))
    shapes, specs = emitted(width, 2, 0)
    outs = pl.pallas_call(
        forward_far_kernel,
        out_shape=[jax.ShapeDtypeStruct((2 * ROWS, hid), F32)] * 2 + shapes,
        grid_spec=pltpu.PrefetchScalarGridSpec(
            num_scalar_prefetch=1,
            grid=(6,),
            in_specs=[whole(r.shape) for r in rows]
            + [far_w, far_w, half_rows, half_rows, pl.BlockSpec(memory_space=pl.ANY)],
            out_specs=[half_rows] * 2 + specs,
            scratch_shapes=[
                pltpu.VMEM((2 * ROWS, hid), BF16),
                pltpu.VMEM((hid, width), BF16),
                pltpu.SemaphoreType.DMA,
            ],
        ),
        compiler_params=params(63),
        cost_estimate=cost(6 * ROWS * width * hid, 2 * width * ROWS + 4 * width * hid + 16 * ROWS * hid),
        name="forward_far",
    )(place, *rows, w_gate, w_up, gate, up, w_down)
    return outs[0], outs[1], (outs[2:7], outs[7:])


def backward(place, rows, w_gate, w_up, w_down, to_gate, to_up):
    hid, width = w_down.shape
    count = 2 * ROWS
    block = width // STEPS
    rows = rows.reshape(GROUPS, 2, ROWS // GROUPS, width)
    shapes, specs = emitted(width, STEPS, 1)
    outs = pl.pallas_call(
        backward_kernel,
        out_shape=shapes,
        grid_spec=pltpu.PrefetchScalarGridSpec(
            num_scalar_prefetch=1,
            grid=(STEPS + 4,),
            in_specs=[
                pl.BlockSpec((*rows.shape[:3], block), lambda i, place: (0, 0, 0, jnp.minimum(i, STEPS - 1))),
                pl.BlockSpec((hid, block), lambda i, place: (0, jnp.minimum(i, STEPS - 1))),
                whole((count, hid)),
                whole((count, hid)),
                ANYWHERE,
                ANYWHERE,
            ],
            out_specs=specs,
            scratch_shapes=[
                pltpu.VMEM((count, hid), F32),
                pltpu.VMEM((count, 2 * hid), BF16),
                pltpu.VMEM((width, 2 * hid), BF16),
                pltpu.SemaphoreType.DMA((2,)),
            ],
        ),
        compiler_params=params(),
        cost_estimate=cost(6 * count * width * hid, 4 * width * count + 6 * width * hid),
        name="backward",
    )(place, rows, w_down, to_gate, to_up, w_gate, w_up)
    return outs[:5], outs[5:]


def combine_kernel(target, weights, *refs):
    homes, mixed = refs[:-1], refs[-1]
    tokens, part = mixed.shape[2:]
    total = jnp.zeros((tokens, part), F32)
    for h, home in enumerate(homes):
        rows = home[:, 0].reshape(-1, part)
        slot = slot_at(lax.broadcasted_iota(jnp.int32, (tokens, rows.shape[0]), 1) & (ROWS - 1), h)
        for k in range(2):
            choose = jnp.where(target[:, k : k + 1] == slot, 1.0, 0.0).astype(BF16)
            total += weights[:, k : k + 1] * dot(choose, rows)
    for copy in range(mixed.shape[0]):
        mixed[copy, 0] = total.astype(BF16)


def combine(homes, target, weights, copies):
    tokens = target.shape[0]
    terms, _, slots, part = homes[0].shape
    return pl.pallas_call(
        combine_kernel,
        out_shape=jax.ShapeDtypeStruct((copies, 2, tokens, part), BF16),
        grid=(2,),
        in_specs=[whole(target.shape), whole(weights.shape)]
        + [pl.BlockSpec((terms, 1, slots, part), lambda n: (0, n, 0, 0)) for _ in homes],
        out_specs=pl.BlockSpec((copies, 1, tokens, part), lambda n: (0, n, 0, 0)),
        compiler_params=params(24),
        cost_estimate=cost(8 * tokens * homes[0].size, 4 * homes[0].size + 4 * copies * tokens * part),
        name="combine",
    )(target, weights, *homes)


def add(*terms):
    return sum(t.astype(F32) for t in terms).astype(BF16)


def later_kernel(block, *refs):
    owns, gots, sends, (mine, came, in_sems, out_sems) = refs[:4], refs[4:8], refs[-8:-4], refs[-4:]
    loads, stores = [], []
    for n in range(4):
        loads.append(
            [
                pltpu.make_async_copy(owns[n], mine.at[n], in_sems.at[0, n]),
                pltpu.make_async_copy(gots[n].at[0], came.at[n], in_sems.at[1, n]),
            ]
        )
        to = sends[n] if block is None else sends[n].at[block]
        stores.append(pltpu.make_async_copy(mine.at[n], to, out_sems.at[n]))
        for load in loads[n]:
            load.start()
    for n in range(4):
        for load in loads[n]:
            load.wait()
        mine[n] = add(mine[n], came[n])
        stores[n].start()
    for store in stores:
        store.wait()


def later_scratch(half):
    return [pltpu.VMEM((4, *half), BF16)] * 2 + [pltpu.SemaphoreType.DMA((2, 4)), pltpu.SemaphoreType.DMA((4,))]


def total_kernel(*refs):
    half = ROWS // 2
    for h in range(2):
        own, first_plus, first_minus, later_plus, later_minus = (r[...] for r in refs[5 * h : 5 * h + 5])
        total = refs[-2 + h]
        first_plus, first_minus, later_plus, later_minus = (
            r.reshape(-1, half, r.shape[-1]) for r in (first_plus, first_minus, later_plus, later_minus)
        )
        shape = (GROUPS // 2, *total.shape[3:])
        for j in range(own.shape[0]):
            top = add(own[j, :half], later_plus[j], first_minus[j])
            bottom = add(own[j, half:], first_plus[j], later_minus[j])
            total[j, : GROUPS // 2, 0] = top.reshape(shape)
            total[j, GROUPS // 2 :, 0] = bottom.reshape(shape)


def both_ways(plus, minus):
    return [shift(p, axis, 1) for p, axis in zip(plus, AXES)] + [shift(m, axis, -1) for m, axis in zip(minus, AXES)]


def ring_join(parts, first, plus, minus):
    half = parts[0][2].shape
    buffers = [*plus, *minus]
    outs = pl.pallas_call(
        functools.partial(later_kernel, 2),
        out_shape=[jax.ShapeDtypeStruct(b.shape, BF16) for b in buffers],
        in_specs=[ANYWHERE] * 12,
        out_specs=[ANYWHERE] * 4,
        scratch_shapes=later_scratch(half),
        input_output_aliases={8 + n: n for n in range(4)},
        compiler_params=params(),
        cost_estimate=cost(0, 24 * half[0] * half[1] * half[2]),
        name="ring_join",
    )(*[p[2] for p in parts], *[p[3] for p in parts], *first, *buffers)
    return outs[:2], outs[2:]


def ring_later(parts, first):
    half = parts[0][2].shape
    outs = pl.pallas_call(
        functools.partial(later_kernel, None),
        out_shape=[jax.ShapeDtypeStruct(half, BF16)] * 4,
        in_specs=[ANYWHERE] * 8,
        out_specs=[ANYWHERE] * 4,
        scratch_shapes=later_scratch(half),
        compiler_params=params(),
        cost_estimate=cost(0, 24 * half[0] * half[1] * half[2]),
        name="ring_later",
    )(*[p[2] for p in parts], *[p[3] for p in parts], *first)
    return outs[:2], outs[2:]


def ring_end(parts, first, later, totals):
    _, rows, part = parts[0][4].shape
    own = pl.BlockSpec((RING, rows, part), lambda j: (j, 0, 0))
    blocks = [pl.BlockSpec((1, RING, rows // 2, part), lambda j, n=n: (n, j, 0, 0)) for n in range(3)]
    last = blocks[2] if totals is None else pl.BlockSpec((RING, rows // 2, part), lambda j: (j, 0, 0))
    operands, specs = [], []
    for h in range(2):
        operands += [parts[h][4], first[h], first[2 + h], later[h], later[2 + h]]
        specs += [own, blocks[1], blocks[1], last, last]
    number = 0 if totals is None else 1
    shape = (RING, GROUPS, 2, rows // GROUPS, part)
    return pl.pallas_call(
        total_kernel,
        out_shape=[jax.ShapeDtypeStruct(shape, BF16)] * 2,
        grid=(1,),
        in_specs=specs + [ANYWHERE] * (2 * number),
        out_specs=[pl.BlockSpec((RING, GROUPS, 1, *shape[3:]), lambda j: (j, 0, number, 0, 0))] * 2,
        input_output_aliases={10 + h: h for h in range(2 * number)},
        compiler_params=params(),
        cost_estimate=cost(0, 16 * RING * rows * part),
        name="ring_end",
    )(*operands, *(totals or ()))


def assemble_kernel(slices, *results):
    count, _, _, part = slices.shape
    for n, result in enumerate(results):
        for c in range(count):
            result[:, c * part : (c + 1) * part] = slices[c, n]


def assemble(slices):
    count, _, tokens, part = slices.shape
    return pl.pallas_call(
        assemble_kernel,
        out_shape=[jax.ShapeDtypeStruct((tokens, count * part), BF16)] * 2,
        grid=(2,),
        in_specs=[pl.BlockSpec((count // 2, 2, tokens, part), lambda i: (i, 0, 0, 0))],
        out_specs=[pl.BlockSpec((tokens, count // 2 * part), lambda i: (0, i))] * 2,
        compiler_params=params(58),
        cost_estimate=cost(0, 4 * slices.size),
        name="assemble",
    )(slices)


def per_device(tokens, routes, route_weights, out_grad, w_gate, w_up, w_down):
    count_rows, width = tokens.shape
    half = ROWS // GROUPS
    chunk = width // RING
    part = chunk // RING
    w_gate, w_up, w_down = w_gate[0], w_up[0], w_down[0]
    places = jnp.stack([lax.axis_index(axis) for axis in AXES]).astype(jnp.int32)

    def to_experts(rows):
        return lax.all_to_all(rows, EXPERT, split_axis=0, concat_axis=0, tiled=True)

    quarters, target = dispatch(places, routes, tokens)
    got = to_experts(quarters)
    every = jnp.arange(2 * ROWS, dtype=jnp.int32)[:, None]
    chosen = ((every == target[None, :, 0]) | (every == target[None, :, 1])).astype(BF16)
    rows_g = to_experts(dot(chosen, out_grad).astype(BF16))
    near, far = gathered([got[:, h].reshape(ROWS, chunk) for h in range(2)])
    to_gate, to_up, out_parts = forward(places, near, far, w_gate, w_up, w_down)
    out_first = both_ways([p[0] for p in out_parts], [p[1] for p in out_parts])
    grad_parts = backward(places, rows_g, w_gate, w_up, w_down, to_gate, to_up)
    plus, minus = ring_join(out_parts, out_first, [p[0] for p in grad_parts], [p[1] for p in grad_parts])
    got = both_ways(plus, minus)
    grad_later = both_ways(*ring_later(grad_parts, got))
    totals = ring_end(out_parts, out_first, got, None)
    totals = ring_end(grad_parts, got, grad_later, totals)
    homes = []
    for h in range(2):
        pieces = totals[h].reshape(RING * GROUPS, 2, half, part)
        axes = (AXES[1 - h], *EXPERT)
        homes.append(lax.all_to_all(pieces, axes, split_axis=0, concat_axis=0, tiled=True))
    copies = combine(homes, target, route_weights, RING * RING)
    moe_out, input_grad = assemble(lax.all_to_all(copies, AXES, split_axis=0, concat_axis=0, tiled=True))
    return moe_out, input_grad


def solution(mesh):
    fine = Mesh(mesh.devices.reshape(4, 2, 4, 4), ("z", "core", "y", "x"))
    row = P(EXPERT, None)
    wide = P(EXPERT, None, ("y", "x"))
    tall = P(EXPERT, ("y", "x"), None)
    return jax.shard_map(
        per_device,
        mesh=fine,
        in_specs=(row, row, row, row, wide, wide, tall),
        out_specs=(row, row),
        check_vma=False,
    )
```
